256 devices in a mesh: ctx: 32 (over z, y_lo, core), head: 8 (over y_hi, x).
Axes of the slice: x: 4, y: 4 (y_hi: 2, y_lo: 2; y = y_hi * 2 + y_lo), z: 8, core: 2. Of those that a mesh axis runs over, the one named last changes fastest.
Arguments:
- queries: bfloat16 [6144, 3072], P('ctx', 'head'), may hold values from -6 to 6
- keys: bfloat16 [6144, 3072], P('ctx', 'head'), may hold values from -6 to 6
- values: bfloat16 [6144, 3072], P('ctx', 'head'), may hold values from -6 to 6
- query_tan: bfloat16 [6144, 3072], P('ctx', 'head'), may hold values from -6 to 6
- key_tan: bfloat16 [6144, 3072], P('ctx', 'head'), may hold values from -6 to 6
- value_tan: bfloat16 [6144, 3072], P('ctx', 'head'), may hold values from -6 to 6
- out_weight: bfloat16 [3072, 5120], P('head'), may hold values from -0.109375 to 0.109375
- gate: float32 [5120], P('head'), may hold values from 8 to 64
- gate_tan: float32 [5120], P('head'), may hold values from -96 to 96
Outputs:
- update: bfloat16 [6144, 5120], P('ctx', 'head')
- update_tan: bfloat16 [6144, 5120], P('ctx', 'head')
The draws below stay inside these ranges and needn't reach their ends.
All inputs are finite; a program needn't handle non-finite values.
Results may differ from the reference program's by a relative error of at most 0.018.
Values may be sent and summed in bfloat16 or wider, within the bound.
A program may use at most 128 MiB of HBM per device.

```python
import math
import jax
import jax.numpy as jnp
from jax import lax

D = 5120
HEADS = 24
DH = 128
HD = 3072
TOKENS = 6144
N_HEAD = 8


def draw_queries(key, part):
    key = jax.random.fold_in(key, 31)
    normal_key = jax.random.fold_in(key, 0)
    sample = jax.random.normal(normal_key, (TOKENS, HEADS * DH), jnp.float32)
    return jnp.clip(sample, -6.0, 6.0).astype(jnp.bfloat16)


def draw_keys(key, part):
    key = jax.random.fold_in(key, 47)
    normal_key = jax.random.fold_in(key, 0)
    sample = jax.random.normal(normal_key, (TOKENS, HEADS * DH), jnp.float32)
    return jnp.clip(sample, -6.0, 6.0).astype(jnp.bfloat16)


def block_scale(rng, dims, cuts, smallest, top_value):
    def one(dim, shards_of):
        steps = jax.random.uniform(jax.random.fold_in(jax.random.fold_in(rng, 6), dim), (shards_of,), jnp.float32, smallest / len(cuts), top_value / len(cuts))
        return jnp.repeat(jnp.exp(steps), dims[dim] // shards_of).reshape((-1,) + (1,) * (len(dims) - dim - 1))

    factor_of = one(*cuts[0])
    for cut in cuts[1:]:
        factor_of = factor_of * one(*cut)
    return factor_of


def normal_values(stream_key, shape, scale, most, shards=(), kind=jnp.bfloat16):
    loudness = block_scale(stream_key, shape, shards, -0.22, 0.18) if shards else 1.0
    entries = jax.random.normal(stream_key, shape, jnp.float32) * scale * loudness
    return jnp.minimum(jnp.maximum(entries, -most), most).astype(kind)


def setup_inputs(seed: int = 0) -> dict:
    seeds = jax.random.split(jax.random.key(seed), 10)
    queries = draw_queries(jax.random.fold_in(seeds[9], 71), 0)
    keys = draw_keys(jax.random.fold_in(seeds[9], 71), 0)
    values = normal_values(seeds[2], (TOKENS, HD), 1.0, 6.0, ((0, 32), (1, 8)))
    query_tan = normal_values(seeds[3], (TOKENS, HD), 1.0, 6.0, ((0, 32), (1, 8)))
    key_tan = normal_values(seeds[4], (TOKENS, HD), 1.0, 6.0, ((0, 32), (1, 8)))
    value_tan = normal_values(seeds[5], (TOKENS, HD), 1.0, 6.0, ((0, 32), (1, 8)))
    out_weight = normal_values(seeds[6], (HD, D), HD ** -0.5, 0.109375, ((0, 8),))
    gate = jnp.clip(jnp.exp(math.log(64.0) - 2.0794415 * jax.random.uniform(seeds[7], (D,), jnp.float32) ** block_scale(seeds[7], (D,), ((0, 8),), -0.2, 0.2)), 8.0, 64.0)
    gate_tan = normal_values(seeds[8], (D,), 16.0, 96.0, ((0, 8),), jnp.float32)
    return {"queries": queries, "keys": keys, "values": values, "query_tan": query_tan, "key_tan": key_tan, "value_tan": value_tan, "out_weight": out_weight, "gate": gate, "gate_tan": gate_tan}


def one_head(head_parts):
    query_head, key_head, value_head, query_tan_head, key_tan_head, value_tan_head = head_parts
    factor = 1.0 / math.sqrt(DH)
    exact = lax.Precision.HIGHEST
    scores = jnp.dot(query_head, key_head.T, precision=exact) * factor
    score_tan = (jnp.dot(query_tan_head, key_head.T, precision=exact) + jnp.dot(query_head, key_tan_head.T, precision=exact)) * factor
    row_max = lax.optimization_barrier(jnp.max(scores, axis=1, keepdims=True))
    exponent = jnp.exp(scores - row_max)
    normalizer = lax.optimization_barrier(jnp.sum(exponent, axis=1, keepdims=True))
    mixed_terms = exponent * score_tan
    slope_mean = lax.optimization_barrier(jnp.sum(mixed_terms, axis=1, keepdims=True)) / normalizer
    weights = lax.optimization_barrier(exponent.astype(jnp.bfloat16)).astype(jnp.float32)
    mixed_weights = lax.optimization_barrier(mixed_terms.astype(jnp.bfloat16)).astype(jnp.float32)
    attention = jnp.dot(weights, value_head, precision=exact) / normalizer
    attention_tan = (jnp.dot(weights, value_tan_head, precision=exact) + jnp.dot(mixed_weights, value_head, precision=exact)) / normalizer - attention * slope_mean
    return (attention.astype(jnp.bfloat16), attention_tan.astype(jnp.bfloat16))

def to_heads(array):
    return array.reshape(TOKENS, HEADS, DH).transpose(1, 0, 2).astype(jnp.float32)

def from_heads(array):
    return array.transpose(1, 0, 2).reshape(TOKENS, HEADS * DH)

def reference(queries, keys, values, query_tan, key_tan, value_tan, out_weight, gate, gate_tan):
    stacked_parts = (to_heads(queries), to_heads(keys), to_heads(values), to_heads(query_tan), to_heads(key_tan), to_heads(value_tan))
    attention, attention_tan = lax.map(one_head, stacked_parts)
    attention = from_heads(attention).astype(jnp.float32)
    attention_tan = from_heads(attention_tan).astype(jnp.float32)
    exact = lax.Precision.HIGHEST
    group_cols = HEADS * DH // N_HEAD
    weight_float = out_weight.astype(jnp.float32)
    projected = jnp.zeros((TOKENS, D), jnp.float32)
    projected_tan = jnp.zeros((TOKENS, D), jnp.float32)
    for group_index in range(N_HEAD):
        first_col = group_index * group_cols
        weight_rows = weight_float[first_col:first_col + group_cols]
        partial_value = jnp.dot(attention[:, first_col:first_col + group_cols], weight_rows, precision=exact)
        partial_tan = jnp.dot(attention_tan[:, first_col:first_col + group_cols], weight_rows, precision=exact)
        projected = projected + lax.optimization_barrier(partial_value.astype(jnp.bfloat16)).astype(jnp.float32)
        projected_tan = projected_tan + lax.optimization_barrier(partial_tan.astype(jnp.bfloat16)).astype(jnp.float32)
    update = (gate[None, :] * projected).astype(jnp.bfloat16)
    update_tan = (gate_tan[None, :] * projected + gate[None, :] * projected_tan).astype(jnp.bfloat16)
    return (update, update_tan)
```

```python
import functools
import math

import jax
import jax.numpy as jnp
from jax import lax
from jax.experimental import pallas as pl
from jax.experimental.pallas import tpu as pltpu
from jax.sharding import PartitionSpec as P

DH = 128
HEADS = 3
RING = 8
WIDE = 4
FACTOR = 1.0 / math.sqrt(DH)
BASE2 = FACTOR * math.log2(math.e)
MESH = pl.DeviceIdType.MESH
F32 = jnp.float32
BF16 = jnp.bfloat16
NT = (((1,), (1,)), ((), ()))
NN = (((1,), (0,)), ((), ()))


def kernel(
    rows,
    width,
    queries,
    keys,
    values,
    query_tan,
    key_tan,
    value_tan,
    out_weight,
    gate,
    gate_tan,
    update,
    update_tan,
    qq,
    kv,
    wbuf,
    abuf,
    top,
    norm,
    slope,
    total,
    own,
    own_lse,
    own_slope,
    part,
    part_got,
    stat,
    stat_got,
    acc,
    load_sem,
    q_sem,
    ring_send,
    ring_recv,
    sib_send,
    sib_recv,
    first_sem,
    w_send,
    w_recv,
    w_sib_send,
    w_sib_recv,
    part_sem,
    att_send,
    att_recv,
):
    half = rows // 2
    i = lax.axis_index("ctx")
    g = lax.axis_index("head")
    z, y, c = i // 4, (i // 2) % 2, i % 2
    yh, x = g // WIDE, g % WIDE
    ahead = (((z + 1) % RING) * 4 + y * 2 + c, g)
    behind = (((z + RING - 1) % RING) * 4 + y * 2 + c, g)
    sibling = (z * 4 + y * 2 + 1 - c, g)
    partner = (z * 4 + (1 - y) * 2 + c, g)

    def peer(r):
        return (i, ((yh + r // WIDE) % 2) * WIDE + (x + r % WIDE) % WIDE)

    def back(r):
        return (r // WIDE) * WIDE + (WIDE - r % WIDE) % WIDE

    loads = []

    def load(src, dst):
        copy = pltpu.make_async_copy(src, dst, load_sem.at[len(loads)])
        copy.start()
        loads.append(copy)

    def cols(h):
        return pl.ds(h * DH, DH)

    for h in range(HEADS):
        for pair, low, high in ((0, keys, key_tan), (1, values, value_tan)):
            load(low.at[:, cols(h)], kv.at[0, h, pair, c, :, pl.ds(0, DH)])
            load(high.at[:, cols(h)], kv.at[0, h, pair, c, :, pl.ds(DH, DH)])
    for h in range(HEADS):
        load(query_tan.at[:, cols(h)], qq.at[h, 0, :, pl.ds(0, DH)])
        load(queries.at[:, cols(h)], qq.at[h, 0, :, pl.ds(DH, DH)])
    load(out_weight.at[:, :, pl.ds(pl.multiple_of(g * width, 128), width)], wbuf.at[:, 0])

    barrier = pltpu.get_barrier_semaphore()
    others = [ahead, behind, sibling, partner] + [peer(r) for r in range(1, 2 * WIDE)]
    for other in others:
        pl.semaphore_signal(barrier, inc=1, device_id=other, device_id_type=MESH)
    pl.semaphore_wait(barrier, len(others))

    def remote(src, dst, send, recv, device):
        return pltpu.make_async_remote_copy(
            src_ref=src,
            dst_ref=dst,
            send_sem=send,
            recv_sem=recv,
            device_id=device,
            device_id_type=MESH,
        )

    def slot_of(d, s):
        return 0 if s == 0 else (7 if s == 4 else 2 * s - 1 + d)

    def piece(d, h, s, part_index):
        return kv.at[slot_of(d, s), h, :, c, pl.ds(part_index * half, half)]

    def ring(d, h, s, p):
        tag = 2 * (s - 1) + (p if s < 4 else 0)
        return remote(
            piece(d, h, s - 1, p),
            piece(d, h, s, p),
            ring_send.at[d, h, tag],
            ring_recv.at[d, h, tag],
            ahead if d == 0 else behind,
        )

    def twin(d, h, s, p):
        tag = 2 * (s - 1) + (p if s < 4 else 0)
        ref = piece(d, h, s, p)
        return remote(ref, ref, sib_send.at[d, h, tag], sib_recv.at[d, h, tag], sibling)

    def twin_got(d, h, s, p):
        tag = 2 * (s - 1) + (p if s < 4 else 0)
        ref = kv.at[slot_of(d, s), h, :, 1 - c, pl.ds(p * half, half)]
        return remote(ref, ref, sib_send.at[d, h, tag], sib_recv.at[d, h, tag], sibling)

    def first(h, core):
        ref = kv.at[0, h, :, core]
        return remote(ref, ref, first_sem.at[0, h], first_sem.at[1, h], sibling)

    def query_copy():
        return remote(qq.at[:, 0], qq.at[:, 1], q_sem.at[0], q_sem.at[1], partner)

    share = DH // 2

    def weight(r):
        column = peer(r)[1] * width
        return remote(
            out_weight.at[:, pl.ds(c * share, share), pl.ds(pl.multiple_of(column, 128), width)],
            wbuf.at[:, back(r), pl.ds(c * share, share)],
            w_send.at[r],
            w_recv.at[back(r)],
            peer(r),
        )

    def weight_got(r):
        ref = wbuf.at[:, r, pl.ds(c * share, share)]
        return remote(ref, ref, w_send.at[r], w_recv.at[r], peer(r))

    def weight_twin(r, core):
        ref = wbuf.at[:, r, pl.ds(core * share, share)]
        return remote(ref, ref, w_sib_send.at[r], w_sib_recv.at[r], sibling)

    def part_copies(h):
        return (
            remote(part.at[h], part_got.at[h], part_sem.at[0, h, 0], part_sem.at[1, h, 0], partner),
            remote(stat.at[h], stat_got.at[h], part_sem.at[0, h, 1], part_sem.at[1, h, 1], partner),
        )

    def attention_copy(h, r):
        return remote(
            abuf.at[h, :, :, pl.ds(0, DH)],
            abuf.at[h, :, :, pl.ds(back(r) * DH, DH)],
            att_send.at[h, r],
            att_recv.at[h, back(r)],
            peer(r),
        )

    def attention_got(h, r):
        ref = abuf.at[h, :, :, pl.ds(r * DH, DH)]
        return remote(ref, ref, att_send.at[h, r], att_recv.at[h, r], peer(r))

    def order(d):
        return ((d, d), (d, 1 - d))

    def begin(h, which):
        for d in range(2):
            ring(d, h, 1, order(d)[which][1]).start()

    def pass_on(h, s):
        for which in range(2):
            for d in range(2):
                p = order(d)[which][1]
                if s == 4 and which == 1:
                    continue
                ring(d, h, s, p).wait_recv()
                if s < 3 or (s == 3 and which == 0):
                    ring(d, h, s + 1, p).start()
                twin(d, h, s, p).start()

    def twins_arrived(h, s):
        for d in range(2):
            for which in range(1 if s == 4 else 2):
                twin_got(d, h, s, order(d)[which][1]).wait_recv()

    def attend(h, slot):
        q = qq[h].reshape(2 * rows, 2 * DH)
        k = kv[slot, h, 0].reshape(2 * rows, 2 * DH)
        v = kv[slot, h, 1].reshape(2 * rows, 2 * DH)
        scores = lax.dot_general(q[:, DH:], k[:, :DH], NT, preferred_element_type=F32)
        score_tan = lax.dot_general(q, k, NT, preferred_element_type=F32)
        old = top[...]
        new = jnp.maximum(old, jnp.max(scores, axis=1, keepdims=True))
        top[...] = new
        alpha = jnp.exp2((old - new) * BASE2)
        weights, mixed = [], []
        for j in range(2 * rows // DH):
            block = slice(j * DH, (j + 1) * DH)
            exponent = jnp.exp2((scores[:, block] - new) * BASE2)
            weights.append(exponent)
            mixed.append(exponent * score_tan[:, block])
        norm[...] = alpha * norm[...] + functools.reduce(jnp.add, weights)
        slope[...] = alpha * slope[...] + functools.reduce(jnp.add, mixed)
        weights = jnp.concatenate([w.astype(BF16) for w in weights], axis=1)
        mixed = jnp.concatenate([w.astype(BF16) for w in mixed], axis=1)
        plain = lax.dot_general(weights, v, NN, preferred_element_type=F32)
        cross = lax.dot_general(mixed, v[:, :DH], NN, preferred_element_type=F32)
        total[0] = alpha * total[0] + plain[:, :DH]
        total[1] = alpha * total[1] + (plain[:, DH:] + FACTOR * cross)

    def finish(h):
        normalizer = jnp.sum(norm[...], axis=1, keepdims=True)
        inverse = 1.0 / normalizer
        slope_mean = FACTOR * jnp.sum(slope[...], axis=1, keepdims=True) * inverse
        plain = total[0] * inverse
        tan = total[1] * inverse - plain * slope_mean
        lse = top[...] * BASE2 + jnp.log2(normalizer)
        own[0] = plain[:rows]
        own[1] = tan[:rows]
        own_lse[...] = lse[:rows]
        own_slope[...] = jnp.broadcast_to(slope_mean[:rows], (rows, DH))
        part[h, 0] = plain[rows:].astype(BF16)
        part[h, 1] = tan[rows:].astype(BF16)
        lane = lax.broadcasted_iota(jnp.int32, (rows, DH), 1)
        both = jnp.where(lane == 0, lse[rows:], slope_mean[rows:])
        both = jnp.concatenate([both, jnp.zeros((256 - rows, DH), F32)], axis=0)
        stat[h] = both.T[:8]
        for copy in part_copies(h):
            copy.start()

    def combine(h):
        for copy in part_copies(h):
            copy.wait_recv()
        both = jnp.concatenate([stat_got[h], jnp.zeros((DH - 8, 256), F32)], axis=0).T
        lse1, slope1 = both[:rows, 0:1], both[:rows, 1:2]
        lse0, slope0 = own_lse[...], own_slope[...]
        most = jnp.maximum(lse0, lse1)
        e0, e1 = jnp.exp2(lse0 - most), jnp.exp2(lse1 - most)
        inverse = 1.0 / (e0 + e1)
        w0, w1 = e0 * inverse, e1 * inverse
        a0, a1 = own[0], part_got[h, 0].astype(F32)
        t0, t1 = own[1], part_got[h, 1].astype(F32)
        abuf[h, 0, :, :DH] = (w0 * a0 + w1 * a1).astype(BF16)
        tan = w0 * t0 + w1 * t1 + (w0 * w1) * (slope0 - slope1) * (a0 - a1)
        abuf[h, 1, :, :DH] = tan.astype(BF16)
        for r in range(1, 2 * WIDE):
            attention_copy(h, r).start()

    def project(h):
        for r in range(1, 2 * WIDE):
            attention_got(h, r).wait_recv()
        left = abuf[h].reshape(2 * rows, 2 * WIDE * DH)
        right = wbuf[h].reshape(2 * WIDE * DH, width)
        acc[...] += lax.dot_general(left, right, NN, preferred_element_type=F32)

    for copy in loads[: 4 * HEADS]:
        copy.wait()
    begin(0, 0)
    begin(0, 1)
    for copy in loads[4 * HEADS : 6 * HEADS]:
        copy.wait()
    query_copy().start()
    for h in range(HEADS):
        first(h, c).start()
    acc[...] = jnp.zeros_like(acc)
    loads[-1].wait()
    weight(1).start()
    weight(4).start()
    pass_on(0, 1)
    query_copy().wait_recv()

    def step(t, carry):
        h, slot = t // RING, t % RING

        @pl.when(slot == 0)
        def _():
            top[...] = jnp.full_like(top, -1e30)
            norm[...] = jnp.zeros_like(norm)
            slope[...] = jnp.zeros_like(slope)
            total[...] = jnp.zeros_like(total)
            first(h, 1 - c).wait_recv()

        @pl.when((slot == 0) & (h < HEADS - 1))
        def _():
            begin(h + 1, 0)

        @pl.when(slot == 1)
        def _():
            pass_on(h, 2)

        @pl.when((slot == 1) & (h < HEADS - 1))
        def _():
            begin(h + 1, 1)

        @pl.when(slot == 1)
        def _():
            twins_arrived(h, 1)

        @pl.when(t == 2)
        def _():
            weight(3).start()
            weight(5).start()

        @pl.when(slot == 3)
        def _():
            twins_arrived(h, 2)

        @pl.when((slot == 4) & (h > 0))
        def _():
            combine(h - 1)

        @pl.when(t == 4)
        def _():
            weight(2).start()
            weight(7).start()

        @pl.when(slot == 5)
        def _():
            pass_on(h, 3)
            twins_arrived(h, 3)

        @pl.when(t == 6)
        def _():
            weight(6).start()

        @pl.when(t == RING + 2)
        def _():
            for r in range(1, 2 * WIDE):
                weight_got(r).wait_recv()
                weight_twin(r, c).start()

        @pl.when((slot == 7) & (h < HEADS - 1))
        def _():
            pass_on(h + 1, 1)

        @pl.when(slot == 7)
        def _():
            pass_on(h, 4)
            twins_arrived(h, 4)

        attend(h, slot)

        @pl.when(slot == 7)
        def _():
            finish(h)

        @pl.when(t == 2 * RING - 1)
        def _():
            for r in range(1, 2 * WIDE):
                weight_twin(r, 1 - c).wait_recv()

        @pl.when((slot == 7) & (h > 0))
        def _():
            project(h - 1)

        return carry

    lax.fori_loop(0, HEADS * RING, step, 0)
    combine(HEADS - 1)
    project(HEADS - 1)

    scale = gate[...]
    projected = acc[:rows]
    update[...] = (scale * projected).astype(BF16)
    update_tan[...] = (gate_tan[...] * projected + scale * acc[rows:]).astype(BF16)

    query_copy().wait_send()

    def drain(h, carry):
        first(h, c).wait_send()
        for copy in part_copies(h):
            copy.wait_send()
        for r in range(1, 2 * WIDE):
            attention_copy(h, r).wait_send()
        for s in range(1, 5):
            for d in range(2):
                for which in range(1 if s == 4 else 2):
                    ring(d, h, s, order(d)[which][1]).wait_send()
                    twin(d, h, s, order(d)[which][1]).wait_send()
        return carry

    lax.fori_loop(0, HEADS, drain, 0)
    for r in range(1, 2 * WIDE):
        weight(r).wait_send()
        weight_twin(r, c).wait_send()


def local(queries, keys, values, query_tan, key_tan, value_tan, out_weight, gate, gate_tan):
    rows = queries.shape[0]
    width = gate.shape[0]
    dma = pltpu.SemaphoreType.DMA
    anywhere = pl.BlockSpec(memory_space=pl.ANY)
    vmem = pl.BlockSpec(memory_space=pltpu.VMEM)
    out = jax.ShapeDtypeStruct((rows, width), BF16)
    return pl.pallas_call(
        functools.partial(kernel, rows, width),
        out_shape=(out, out),
        in_specs=[anywhere] * 7 + [vmem] * 2,
        out_specs=(vmem, vmem),
        scratch_shapes=[
            pltpu.VMEM((HEADS, 2, rows, 2 * DH), BF16),
            pltpu.VMEM((RING, HEADS, 2, 2, rows, 2 * DH), BF16),
            pltpu.VMEM((HEADS, 2 * WIDE, DH, width), BF16),
            pltpu.VMEM((HEADS, 2, rows, 2 * WIDE * DH), BF16),
            pltpu.VMEM((2 * rows, DH), F32),
            pltpu.VMEM((2 * rows, DH), F32),
            pltpu.VMEM((2 * rows, DH), F32),
            pltpu.VMEM((2, 2 * rows, DH), F32),
            pltpu.VMEM((2, rows, DH), F32),
            pltpu.VMEM((rows, DH), F32),
            pltpu.VMEM((rows, DH), F32),
            pltpu.VMEM((HEADS, 2, rows, DH), BF16),
            pltpu.VMEM((HEADS, 2, rows, DH), BF16),
            pltpu.VMEM((HEADS, 8, 256), F32),
            pltpu.VMEM((HEADS, 8, 256), F32),
            pltpu.VMEM((2 * rows, width), F32),
            dma((6 * HEADS + 1,)),
            dma((2,)),
            dma((2, HEADS, 7)),
            dma((2, HEADS, 7)),
            dma((2, HEADS, 7)),
            dma((2, HEADS, 7)),
            dma((2, HEADS)),
            dma((2 * WIDE,)),
            dma((2 * WIDE,)),
            dma((2 * WIDE,)),
            dma((2 * WIDE,)),
            dma((2, HEADS, 2)),
            dma((HEADS, 2 * WIDE)),
            dma((HEADS, 2 * WIDE)),
        ],
        compiler_params=pltpu.CompilerParams(
            collective_id=0, has_side_effects=True, vmem_limit_bytes=48 << 20
        ),
    )(
        queries,
        keys,
        values,
        query_tan,
        key_tan,
        value_tan,
        out_weight.reshape(HEADS, DH, -1),
        gate.reshape(1, -1),
        gate_tan.reshape(1, -1),
    )


def solution(mesh):
    token = P("ctx", "head")
    in_specs = (token,) * 6 + (P("head", None), P("head"), P("head"))
    return jax.shard_map(
        local, mesh=mesh, in_specs=in_specs, out_specs=(token, token), check_vma=False
    )
```

```python
import functools
import math

import jax
import jax.numpy as jnp
from jax import lax
from jax.experimental import pallas as pl
from jax.experimental.pallas import tpu as pltpu
from jax.sharding import PartitionSpec as P

DH = 128
HEADS = 3
RING = 8
WIDE = 4
FACTOR = 1.0 / math.sqrt(DH)
BASE2 = FACTOR * math.log2(math.e)
MESH = pl.DeviceIdType.MESH
F32 = jnp.float32
BF16 = jnp.bfloat16
NT = (((1,), (1,)), ((), ()))
NN = (((1,), (0,)), ((), ()))


def kernel(
    rows,
    width,
    queries,
    keys,
    values,
    query_tan,
    key_tan,
    value_tan,
    out_weight,
    acc,
    qq,
    kv,
    wbuf,
    abuf,
    top,
    norm,
    slope,
    total,
    own,
    own_lse,
    own_slope,
    part,
    part_got,
    stat,
    stat_got,
    load_sem,
    q_sem,
    ring_send,
    ring_recv,
    sib_send,
    sib_recv,
    first_sem,
    w_send,
    w_recv,
    w_sib_send,
    w_sib_recv,
    part_sem,
    att_send,
    att_recv,
):
    half = rows // 2
    i = lax.axis_index("ctx")
    g = lax.axis_index("head")
    z, y, c = i // 4, (i // 2) % 2, i % 2
    yh, x = g // WIDE, g % WIDE
    ahead = (((z + 1) % RING) * 4 + y * 2 + c, g)
    behind = (((z + RING - 1) % RING) * 4 + y * 2 + c, g)
    sibling = (z * 4 + y * 2 + 1 - c, g)
    partner = (z * 4 + (1 - y) * 2 + c, g)

    def peer(r):
        return (i, ((yh + r // WIDE) % 2) * WIDE + (x + r % WIDE) % WIDE)

    def back(r):
        return (r // WIDE) * WIDE + (WIDE - r % WIDE) % WIDE

    loads = []

    def load(src, dst):
        copy = pltpu.make_async_copy(src, dst, load_sem.at[len(loads)])
        copy.start()
        loads.append(copy)

    def cols(h):
        return pl.ds(h * DH, DH)

    for h in range(HEADS):
        for pair, low, high in ((0, keys, key_tan), (1, values, value_tan)):
            load(low.at[:, cols(h)], kv.at[0, h, pair, c, :, pl.ds(0, DH)])
            load(high.at[:, cols(h)], kv.at[0, h, pair, c, :, pl.ds(DH, DH)])
    for h in range(HEADS):
        load(query_tan.at[:, cols(h)], qq.at[h, 0, :, pl.ds(0, DH)])
        load(queries.at[:, cols(h)], qq.at[h, 0, :, pl.ds(DH, DH)])
    load(out_weight.at[:, :, pl.ds(pl.multiple_of(g * width, 128), width)], wbuf.at[:, 0])

    barrier = pltpu.get_barrier_semaphore()
    others = [ahead, behind, sibling, partner] + [peer(r) for r in range(1, 2 * WIDE)]
    for other in others:
        pl.semaphore_signal(barrier, inc=1, device_id=other, device_id_type=MESH)
    pl.semaphore_wait(barrier, len(others))

    def remote(src, dst, send, recv, device):
        return pltpu.make_async_remote_copy(
            src_ref=src,
            dst_ref=dst,
            send_sem=send,
            recv_sem=recv,
            device_id=device,
            device_id_type=MESH,
        )

    def slot_of(d, s):
        return 0 if s == 0 else (7 if s == 4 else 2 * s - 1 + d)

    def piece(d, h, s, part_index):
        return kv.at[slot_of(d, s), h, :, c, pl.ds(part_index * half, half)]

    def ring(d, h, s, p):
        tag = 2 * (s - 1) + (p if s < 4 else 0)
        return remote(
            piece(d, h, s - 1, p),
            piece(d, h, s, p),
            ring_send.at[d, h, tag],
            ring_recv.at[d, h, tag],
            ahead if d == 0 else behind,
        )

    def twin(d, h, s, p):
        tag = 2 * (s - 1) + (p if s < 4 else 0)
        ref = piece(d, h, s, p)
        return remote(ref, ref, sib_send.at[d, h, tag], sib_recv.at[d, h, tag], sibling)

    def twin_got(d, h, s, p):
        tag = 2 * (s - 1) + (p if s < 4 else 0)
        ref = kv.at[slot_of(d, s), h, :, 1 - c, pl.ds(p * half, half)]
        return remote(ref, ref, sib_send.at[d, h, tag], sib_recv.at[d, h, tag], sibling)

    def first(h, core):
        ref = kv.at[0, h, :, core]
        return remote(ref, ref, first_sem.at[0, h], first_sem.at[1, h], sibling)

    def query_copy():
        return remote(qq.at[:, 0], qq.at[:, 1], q_sem.at[0], q_sem.at[1], partner)

    share = DH // 2

    def weight(r):
        column = peer(r)[1] * width
        return remote(
            out_weight.at[:, pl.ds(c * share, share), pl.ds(pl.multiple_of(column, 128), width)],
            wbuf.at[:, back(r), pl.ds(c * share, share)],
            w_send.at[r],
            w_recv.at[back(r)],
            peer(r),
        )

    def weight_got(r):
        ref = wbuf.at[:, r, pl.ds(c * share, share)]
        return remote(ref, ref, w_send.at[r], w_recv.at[r], peer(r))

    def weight_twin(r, core):
        ref = wbuf.at[:, r, pl.ds(core * share, share)]
        return remote(ref, ref, w_sib_send.at[r], w_sib_recv.at[r], sibling)

    def part_copies(h):
        return (
            remote(part.at[h], part_got.at[h], part_sem.at[0, h, 0], part_sem.at[1, h, 0], partner),
            remote(stat.at[h], stat_got.at[h], part_sem.at[0, h, 1], part_sem.at[1, h, 1], partner),
        )

    def attention_copy(h, r):
        return remote(
            abuf.at[h, :, :, pl.ds(0, DH)],
            abuf.at[h, :, :, pl.ds(back(r) * DH, DH)],
            att_send.at[h, r],
            att_recv.at[h, back(r)],
            peer(r),
        )

    def attention_got(h, r):
        ref = abuf.at[h, :, :, pl.ds(r * DH, DH)]
        return remote(ref, ref, att_send.at[h, r], att_recv.at[h, r], peer(r))

    def order(d):
        return ((d, d), (d, 1 - d))

    def begin(h, which):
        for d in range(2):
            ring(d, h, 1, order(d)[which][1]).start()

    def pass_on(h, s):
        for which in range(2):
            for d in range(2):
                p = order(d)[which][1]
                if s == 4 and which == 1:
                    continue
                ring(d, h, s, p).wait_recv()
                if s < 3 or (s == 3 and which == 0):
                    ring(d, h, s + 1, p).start()
                twin(d, h, s, p).start()

    def twins_arrived(h, s):
        for d in range(2):
            for which in range(1 if s == 4 else 2):
                twin_got(d, h, s, order(d)[which][1]).wait_recv()

    def attend(h, slot):
        q = qq[h].reshape(2 * rows, 2 * DH)
        k = kv[slot, h, 0].reshape(2 * rows, 2 * DH)
        v = kv[slot, h, 1].reshape(2 * rows, 2 * DH)
        scores = lax.dot_general(q[:, DH:], k[:, :DH], NT, preferred_element_type=F32)
        score_tan = lax.dot_general(q, k, NT, preferred_element_type=F32)
        old = top[...]
        new = jnp.maximum(old, jnp.max(scores, axis=1, keepdims=True))
        top[...] = new
        alpha = jnp.exp2((old - new) * BASE2)
        weights, mixed = [], []
        for j in range(2 * rows // DH):
            block = slice(j * DH, (j + 1) * DH)
            exponent = jnp.exp2((scores[:, block] - new) * BASE2)
            weights.append(exponent)
            mixed.append(exponent * score_tan[:, block])
        norm[...] = alpha * norm[...] + functools.reduce(jnp.add, weights)
        slope[...] = alpha * slope[...] + functools.reduce(jnp.add, mixed)
        weights = jnp.concatenate([w.astype(BF16) for w in weights], axis=1)
        mixed = jnp.concatenate([w.astype(BF16) for w in mixed], axis=1)
        plain = lax.dot_general(weights, v, NN, preferred_element_type=F32)
        cross = lax.dot_general(mixed, v[:, :DH], NN, preferred_element_type=F32)
        total[0] = alpha * total[0] + plain[:, :DH]
        total[1] = alpha * total[1] + (plain[:, DH:] + FACTOR * cross)

    def finish(h):
        normalizer = jnp.sum(norm[...], axis=1, keepdims=True)
        inverse = 1.0 / normalizer
        slope_mean = FACTOR * jnp.sum(slope[...], axis=1, keepdims=True) * inverse
        plain = total[0] * inverse
        tan = total[1] * inverse - plain * slope_mean
        lse = top[...] * BASE2 + jnp.log2(normalizer)
        own[0] = plain[:rows]
        own[1] = tan[:rows]
        own_lse[...] = lse[:rows]
        own_slope[...] = jnp.broadcast_to(slope_mean[:rows], (rows, DH))
        part[h, 0] = plain[rows:].astype(BF16)
        part[h, 1] = tan[rows:].astype(BF16)
        lane = lax.broadcasted_iota(jnp.int32, (rows, DH), 1)
        both = jnp.where(lane == 0, lse[rows:], slope_mean[rows:])
        both = jnp.concatenate([both, jnp.zeros((256 - rows, DH), F32)], axis=0)
        stat[h] = both.T[:8]
        for copy in part_copies(h):
            copy.start()

    def combine(h):
        for copy in part_copies(h):
            copy.wait_recv()
        both = jnp.concatenate([stat_got[h], jnp.zeros((DH - 8, 256), F32)], axis=0).T
        lse1, slope1 = both[:rows, 0:1], both[:rows, 1:2]
        lse0, slope0 = own_lse[...], own_slope[...]
        most = jnp.maximum(lse0, lse1)
        e0, e1 = jnp.exp2(lse0 - most), jnp.exp2(lse1 - most)
        inverse = 1.0 / (e0 + e1)
        w0, w1 = e0 * inverse, e1 * inverse
        a0, a1 = own[0], part_got[h, 0].astype(F32)
        t0, t1 = own[1], part_got[h, 1].astype(F32)
        abuf[h, 0, :, :DH] = (w0 * a0 + w1 * a1).astype(BF16)
        tan = w0 * t0 + w1 * t1 + (w0 * w1) * (slope0 - slope1) * (a0 - a1)
        abuf[h, 1, :, :DH] = tan.astype(BF16)
        for r in range(1, 2 * WIDE):
            attention_copy(h, r).start()

    def project(h):
        for r in range(1, 2 * WIDE):
            attention_got(h, r).wait_recv()
        left = abuf[h].reshape(2 * rows, 2 * WIDE * DH)
        right = wbuf[h].reshape(2 * WIDE * DH, width)
        acc[...] += lax.dot_general(left, right, NN, preferred_element_type=F32)

    for copy in loads[: 4 * HEADS]:
        copy.wait()
    begin(0, 0)
    begin(0, 1)
    for copy in loads[4 * HEADS : 6 * HEADS]:
        copy.wait()
    query_copy().start()
    for h in range(HEADS):
        first(h, c).start()
    acc[...] = jnp.zeros_like(acc)
    loads[-1].wait()
    for r in range(1, 2 * WIDE):
        weight(r).start()
    pass_on(0, 1)
    query_copy().wait_recv()

    def step(t, carry):
        h, slot = t // RING, t % RING

        @pl.when(slot == 0)
        def _():
            top[...] = jnp.full_like(top, -1e30)
            norm[...] = jnp.zeros_like(norm)
            slope[...] = jnp.zeros_like(slope)
            total[...] = jnp.zeros_like(total)
            first(h, 1 - c).wait_recv()

        @pl.when((slot == 0) & (h < HEADS - 1))
        def _():
            begin(h + 1, 0)

        @pl.when(slot == 1)
        def _():
            pass_on(h, 2)

        @pl.when((slot == 1) & (h < HEADS - 1))
        def _():
            begin(h + 1, 1)

        @pl.when(slot == 1)
        def _():
            twins_arrived(h, 1)

        @pl.when((slot == 3) & (h > 0))
        def _():
            combine(h - 1)

        @pl.when(slot == 3)
        def _():
            twins_arrived(h, 2)

        @pl.when(slot == 5)
        def _():
            pass_on(h, 3)
            twins_arrived(h, 3)

        @pl.when(t == 2 * RING - 2)
        def _():
            for r in range(1, 2 * WIDE):
                weight_got(r).wait_recv()
                weight_twin(r, c).start()

        @pl.when(t == 3 * RING - 2)
        def _():
            for r in range(1, 2 * WIDE):
                weight_twin(r, 1 - c).wait_recv()
            project(0)

        @pl.when((slot == 7) & (h < HEADS - 1))
        def _():
            pass_on(h + 1, 1)

        @pl.when(slot == 7)
        def _():
            pass_on(h, 4)
            twins_arrived(h, 4)

        attend(h, slot)

        @pl.when(slot == 7)
        def _():
            finish(h)

        return carry

    lax.fori_loop(0, HEADS * RING, step, 0)
    project(HEADS - 2)
    combine(HEADS - 1)
    project(HEADS - 1)

    query_copy().wait_send()

    def drain(h, carry):
        first(h, c).wait_send()
        for copy in part_copies(h):
            copy.wait_send()
        for r in range(1, 2 * WIDE):
            attention_copy(h, r).wait_send()
        for s in range(1, 5):
            for d in range(2):
                for which in range(1 if s == 4 else 2):
                    ring(d, h, s, order(d)[which][1]).wait_send()
                    twin(d, h, s, order(d)[which][1]).wait_send()
        return carry

    lax.fori_loop(0, HEADS, drain, 0)
    for r in range(1, 2 * WIDE):
        weight(r).wait_send()
        weight_twin(r, c).wait_send()


def local(queries, keys, values, query_tan, key_tan, value_tan, out_weight, gate, gate_tan):
    fixed = (queries, keys, values, query_tan, key_tan, value_tan, out_weight.reshape(HEADS, DH, -1))
    fixed = [pltpu.with_memory_space_constraint(array, pltpu.HBM) for array in fixed]
    rows = queries.shape[0]
    width = gate.shape[0]
    dma = pltpu.SemaphoreType.DMA
    hbm = pl.BlockSpec(memory_space=pltpu.HBM)
    vmem = pl.BlockSpec(memory_space=pltpu.VMEM)
    projected = pl.pallas_call(
        functools.partial(kernel, rows, width),
        out_shape=jax.ShapeDtypeStruct((2 * rows, width), F32),
        in_specs=[hbm] * 7,
        out_specs=vmem,
        scratch_shapes=[
            pltpu.VMEM((HEADS, 2, rows, 2 * DH), BF16),
            pltpu.VMEM((RING, HEADS, 2, 2, rows, 2 * DH), BF16),
            pltpu.VMEM((HEADS, 2 * WIDE, DH, width), BF16),
            pltpu.VMEM((HEADS, 2, rows, 2 * WIDE * DH), BF16),
            pltpu.VMEM((2 * rows, DH), F32),
            pltpu.VMEM((2 * rows, DH), F32),
            pltpu.VMEM((2 * rows, DH), F32),
            pltpu.VMEM((2, 2 * rows, DH), F32),
            pltpu.VMEM((2, rows, DH), F32),
            pltpu.VMEM((rows, DH), F32),
            pltpu.VMEM((rows, DH), F32),
            pltpu.VMEM((HEADS, 2, rows, DH), BF16),
            pltpu.VMEM((HEADS, 2, rows, DH), BF16),
            pltpu.VMEM((HEADS, 8, 256), F32),
            pltpu.VMEM((HEADS, 8, 256), F32),
            dma((6 * HEADS + 1,)),
            dma((2,)),
            dma((2, HEADS, 7)),
            dma((2, HEADS, 7)),
            dma((2, HEADS, 7)),
            dma((2, HEADS, 7)),
            dma((2, HEADS)),
            dma((2 * WIDE,)),
            dma((2 * WIDE,)),
            dma((2 * WIDE,)),
            dma((2 * WIDE,)),
            dma((2, HEADS, 2)),
            dma((HEADS, 2 * WIDE)),
            dma((HEADS, 2 * WIDE)),
        ],
        compiler_params=pltpu.CompilerParams(
            collective_id=0, has_side_effects=True, vmem_limit_bytes=40 << 20
        ),
    )(*fixed)
    plain, tan = projected[:rows], projected[rows:]
    update = (gate[None, :] * plain).astype(BF16)
    update_tan = (gate_tan[None, :] * plain + gate[None, :] * tan).astype(BF16)
    return update, update_tan


def solution(mesh):
    token = P("ctx", "head")
    in_specs = (token,) * 6 + (P("head", None), P("head"), P("head"))
    return jax.shard_map(
        local, mesh=mesh, in_specs=in_specs, out_specs=(token, token), check_vma=False
    )
```

```python
import functools
import math

import jax
import jax.numpy as jnp
from jax import lax
from jax.experimental import pallas as pl
from jax.experimental.pallas import tpu as pltpu
from jax.sharding import PartitionSpec as P

DH = 128
HEADS = 3
RING = 8
WIDE = 4
FACTOR = 1.0 / math.sqrt(DH)
BASE2 = FACTOR * math.log2(math.e)
MESH = pl.DeviceIdType.MESH
F32 = jnp.float32
BF16 = jnp.bfloat16
NT = (((1,), (1,)), ((), ()))
NN = (((1,), (0,)), ((), ()))


def kernel(
    rows,
    width,
    queries,
    keys,
    values,
    query_tan,
    key_tan,
    value_tan,
    out_weight,
    acc,
    qq,
    kv,
    wbuf,
    abuf,
    top,
    norm,
    slope,
    total,
    own,
    own_lse,
    own_slope,
    part,
    part_got,
    stat,
    stat_got,
    load_sem,
    q_sem,
    ring_send,
    ring_recv,
    sib_send,
    sib_recv,
    first_sem,
    w_send,
    w_recv,
    w_sib_send,
    w_sib_recv,
    part_sem,
    att_send,
    att_recv,
):
    half = rows // 2
    i = lax.axis_index("ctx")
    g = lax.axis_index("head")
    z, y, c = i // 4, (i // 2) % 2, i % 2
    yh, x = g // WIDE, g % WIDE
    ahead = (((z + 1) % RING) * 4 + y * 2 + c, g)
    behind = (((z + RING - 1) % RING) * 4 + y * 2 + c, g)
    sibling = (z * 4 + y * 2 + 1 - c, g)
    partner = (z * 4 + (1 - y) * 2 + c, g)

    def peer(r):
        return (i, ((yh + r // WIDE) % 2) * WIDE + (x + r % WIDE) % WIDE)

    def back(r):
        return (r // WIDE) * WIDE + (WIDE - r % WIDE) % WIDE

    barrier = pltpu.get_barrier_semaphore()
    others = [ahead, behind, sibling, partner] + [peer(r) for r in range(1, 2 * WIDE)]
    for other in others:
        pl.semaphore_signal(barrier, inc=1, device_id=other, device_id_type=MESH)

    loads = []

    def load(src, dst):
        copy = pltpu.make_async_copy(src, dst, load_sem.at[len(loads)])
        copy.start()
        loads.append(copy)

    def cols(h):
        return pl.ds(h * DH, DH)

    for h in range(HEADS):
        for pair, low, high in ((0, keys, key_tan), (1, values, value_tan)):
            load(low.at[:, cols(h)], kv.at[0, h, pair, c, :, pl.ds(0, DH)])
            load(high.at[:, cols(h)], kv.at[0, h, pair, c, :, pl.ds(DH, DH)])
    for h in range(HEADS):
        load(query_tan.at[:, cols(h)], qq.at[h, 0, :, pl.ds(0, DH)])
        load(queries.at[:, cols(h)], qq.at[h, 0, :, pl.ds(DH, DH)])
    load(out_weight.at[:, :, pl.ds(pl.multiple_of(g * width, 128), width)], wbuf.at[:, 0])

    pl.semaphore_wait(barrier, len(others))

    def remote(src, dst, send, recv, device):
        return pltpu.make_async_remote_copy(
            src_ref=src,
            dst_ref=dst,
            send_sem=send,
            recv_sem=recv,
            device_id=device,
            device_id_type=MESH,
        )

    def slot_of(d, s):
        return 0 if s == 0 else (7 if s == 4 else 2 * s - 1 + d)

    def piece(d, h, s, part_index):
        return kv.at[slot_of(d, s), h, :, c, pl.ds(part_index * half, half)]

    def ring(d, h, s, p):
        tag = 2 * (s - 1) + (p if s < 4 else 0)
        return remote(
            piece(d, h, s - 1, p),
            piece(d, h, s, p),
            ring_send.at[d, h, tag],
            ring_recv.at[d, h, tag],
            ahead if d == 0 else behind,
        )

    def twin(d, h, s, p):
        tag = 2 * (s - 1) + (p if s < 4 else 0)
        ref = piece(d, h, s, p)
        return remote(ref, ref, sib_send.at[d, h, tag], sib_recv.at[d, h, tag], sibling)

    def twin_got(d, h, s, p):
        tag = 2 * (s - 1) + (p if s < 4 else 0)
        ref = kv.at[slot_of(d, s), h, :, 1 - c, pl.ds(p * half, half)]
        return remote(ref, ref, sib_send.at[d, h, tag], sib_recv.at[d, h, tag], sibling)

    def first(h, core):
        ref = kv.at[0, h, :, core]
        return remote(ref, ref, first_sem.at[0, h], first_sem.at[1, h], sibling)

    def query_copy():
        return remote(qq.at[:, 0], qq.at[:, 1], q_sem.at[0], q_sem.at[1], partner)

    share = DH // 2

    def weight(r):
        column = peer(r)[1] * width
        return remote(
            out_weight.at[:, pl.ds(c * share, share), pl.ds(pl.multiple_of(column, 128), width)],
            wbuf.at[:, back(r), pl.ds(c * share, share)],
            w_send.at[r],
            w_recv.at[back(r)],
            peer(r),
        )

    def weight_got(r):
        ref = wbuf.at[:, r, pl.ds(c * share, share)]
        return remote(ref, ref, w_send.at[r], w_recv.at[r], peer(r))

    def weight_twin(r, core):
        ref = wbuf.at[:, r, pl.ds(core * share, share)]
        return remote(ref, ref, w_sib_send.at[r], w_sib_recv.at[r], sibling)

    def part_copies(h):
        return (
            remote(part.at[h], part_got.at[h], part_sem.at[0, h, 0], part_sem.at[1, h, 0], partner),
            remote(stat.at[h], stat_got.at[h], part_sem.at[0, h, 1], part_sem.at[1, h, 1], partner),
        )

    straight = ((0, 4, 4), (0, 2, 2), (0, 1, 3), (0, 3, 1))
    onward = ((4, 1, 7), (4, 3, 5), (2, 4, 6))

    def attention_copy(h, leg):
        source, target, lands = leg
        return remote(
            abuf.at[h, :, :, pl.ds(source * DH, DH)],
            abuf.at[h, :, :, pl.ds(lands * DH, DH)],
            att_send.at[h, lands],
            att_recv.at[h, lands],
            peer(target),
        )

    def attention_got(h, r):
        ref = abuf.at[h, :, :, pl.ds(r * DH, DH)]
        return remote(ref, ref, att_send.at[h, r], att_recv.at[h, r], peer(r))

    def order(d):
        return ((d, d), (d, 1 - d))

    def begin(h, which):
        for d in range(2):
            ring(d, h, 1, order(d)[which][1]).start()

    def pass_on(h, s):
        for which in range(2):
            for d in range(2):
                p = order(d)[which][1]
                if s == 4 and which == 1:
                    continue
                ring(d, h, s, p).wait_recv()
                if s < 3 or (s == 3 and which == 0):
                    ring(d, h, s + 1, p).start()
                twin(d, h, s, p).start()

    def twins_arrived(h, s):
        for d in range(2):
            for which in range(1 if s == 4 else 2):
                twin_got(d, h, s, order(d)[which][1]).wait_recv()

    def attend(h, slot):
        q = qq[h].reshape(2 * rows, 2 * DH)
        k = kv[slot, h, 0].reshape(2 * rows, 2 * DH)
        v = kv[slot, h, 1].reshape(2 * rows, 2 * DH)
        scores = lax.dot_general(q[:, DH:], k[:, :DH], NT, preferred_element_type=F32)
        score_tan = lax.dot_general(q, k, NT, preferred_element_type=F32)
        old = top[...]
        new = jnp.maximum(old, jnp.max(scores, axis=1, keepdims=True))
        top[...] = new
        alpha = jnp.exp2((old - new) * BASE2)
        weights, mixed = [], []
        for j in range(2 * rows // DH):
            block = slice(j * DH, (j + 1) * DH)
            exponent = jnp.exp2((scores[:, block] - new) * BASE2)
            weights.append(exponent)
            mixed.append(exponent * score_tan[:, block])
        norm[...] = alpha * norm[...] + functools.reduce(jnp.add, weights)
        slope[...] = alpha * slope[...] + functools.reduce(jnp.add, mixed)
        weights = jnp.concatenate([w.astype(BF16) for w in weights], axis=1)
        mixed = jnp.concatenate([w.astype(BF16) for w in mixed], axis=1)
        plain = lax.dot_general(weights, v, NN, preferred_element_type=F32)
        cross = lax.dot_general(mixed, v[:, :DH], NN, preferred_element_type=F32)
        total[0] = alpha * total[0] + plain[:, :DH]
        total[1] = alpha * total[1] + (plain[:, DH:] + FACTOR * cross)

    def finish(h):
        normalizer = jnp.sum(norm[...], axis=1, keepdims=True)
        inverse = 1.0 / normalizer
        slope_mean = FACTOR * jnp.sum(slope[...], axis=1, keepdims=True) * inverse
        plain = total[0] * inverse
        tan = total[1] * inverse - plain * slope_mean
        lse = top[...] * BASE2 + jnp.log2(normalizer)
        own[0] = plain[:rows]
        own[1] = tan[:rows]
        own_lse[...] = lse[:rows]
        own_slope[...] = jnp.broadcast_to(slope_mean[:rows], (rows, DH))
        part[h, 0] = plain[rows:].astype(BF16)
        part[h, 1] = tan[rows:].astype(BF16)
        lane = lax.broadcasted_iota(jnp.int32, (rows, DH), 1)
        both = jnp.where(lane == 0, lse[rows:], slope_mean[rows:])
        both = jnp.concatenate([both, jnp.zeros((256 - rows, DH), F32)], axis=0)
        stat[h] = both.T[:8]
        for copy in part_copies(h):
            copy.start()

    def combine(h):
        for copy in part_copies(h):
            copy.wait_recv()
        both = jnp.concatenate([stat_got[h], jnp.zeros((DH - 8, 256), F32)], axis=0).T
        lse1, slope1 = both[:rows, 0:1], both[:rows, 1:2]
        lse0, slope0 = own_lse[...], own_slope[...]
        most = jnp.maximum(lse0, lse1)
        e0, e1 = jnp.exp2(lse0 - most), jnp.exp2(lse1 - most)
        inverse = 1.0 / (e0 + e1)
        w0, w1 = e0 * inverse, e1 * inverse
        a0, a1 = own[0], part_got[h, 0].astype(F32)
        t0, t1 = own[1], part_got[h, 1].astype(F32)
        abuf[h, 0, :, :DH] = (w0 * a0 + w1 * a1).astype(BF16)
        tan = w0 * t0 + w1 * t1 + (w0 * w1) * (slope0 - slope1) * (a0 - a1)
        abuf[h, 1, :, :DH] = tan.astype(BF16)
        for leg in straight:
            attention_copy(h, leg).start()

    def hand_on(h):
        attention_got(h, 4).wait_recv()
        for leg in onward[:2]:
            attention_copy(h, leg).start()
        attention_got(h, 2).wait_recv()
        attention_copy(h, onward[2]).start()

    def project(h, low, high):
        for r in range(low, high):
            if r not in (0, 2, 4):
                attention_got(h, r).wait_recv()
        left = abuf[h, :, :, low * DH : high * DH].reshape(2 * rows, (high - low) * DH)
        right = wbuf[h, low:high].reshape((high - low) * DH, width)
        acc[...] += lax.dot_general(left, right, NN, preferred_element_type=F32)

    for copy in loads[: 4 * HEADS]:
        copy.wait()
    begin(0, 0)
    begin(0, 1)
    for copy in loads[4 * HEADS : 6 * HEADS]:
        copy.wait()
    query_copy().start()
    for h in range(HEADS):
        first(h, c).start()
    acc[...] = jnp.zeros_like(acc)
    loads[-1].wait()
    pass_on(0, 1)
    query_copy().wait_recv()

    def step(t, carry):
        h, slot = t // RING, t % RING

        @pl.when(slot == 0)
        def _():
            top[...] = jnp.full_like(top, -1e30)
            norm[...] = jnp.zeros_like(norm)
            slope[...] = jnp.zeros_like(slope)
            total[...] = jnp.zeros_like(total)
            first(h, 1 - c).wait_recv()

        @pl.when((slot == 0) & (h < HEADS - 1))
        def _():
            begin(h + 1, 0)

        @pl.when(slot == 1)
        def _():
            pass_on(h, 2)

        @pl.when((slot == 1) & (h < HEADS - 1))
        def _():
            begin(h + 1, 1)

        @pl.when(slot == 1)
        def _():
            twins_arrived(h, 1)

        for r, when in ((6, 0), (5, 1), (7, 2), (4, 3), (2, 4), (1, 5), (3, 6)):

            @pl.when(t == when)
            def _():
                weight(r).start()

        @pl.when(t == 2 * RING + 3)
        def _():
            combine(1)

        @pl.when(slot == 3)
        def _():
            twins_arrived(h, 2)

        @pl.when(slot == 5)
        def _():
            pass_on(h, 3)
            twins_arrived(h, 3)

        @pl.when(t == RING + 5)
        def _():
            combine(0)

        @pl.when(t == 2 * RING + 2)
        def _():
            for r in range(1, 2 * WIDE):
                weight_got(r).wait_recv()
                weight_twin(r, c).start()

        @pl.when(t == 2 * RING + 1)
        def _():
            hand_on(0)

        @pl.when(t == 3 * RING - 2)
        def _():
            hand_on(1)

        @pl.when((slot == 7) & (h < HEADS - 1))
        def _():
            pass_on(h + 1, 1)

        @pl.when(slot == 7)
        def _():
            pass_on(h, 4)
            twins_arrived(h, 4)

        attend(h, slot)

        @pl.when(slot == 7)
        def _():
            finish(h)

        return carry

    lax.fori_loop(0, HEADS * RING, step, 0)
    for r in range(1, 2 * WIDE):
        weight_twin(r, 1 - c).wait_recv()
    project(0, 0, 2 * WIDE)
    combine(2)
    project(1, 0, 2 * WIDE)
    hand_on(2)
    project(2, 0, 5)
    project(2, 5, 2 * WIDE)

    query_copy().wait_send()

    def drain(h, carry):
        first(h, c).wait_send()
        for copy in part_copies(h):
            copy.wait_send()
        for leg in straight + onward:
            attention_copy(h, leg).wait_send()
        for s in range(1, 5):
            for d in range(2):
                for which in range(1 if s == 4 else 2):
                    ring(d, h, s, order(d)[which][1]).wait_send()
                    twin(d, h, s, order(d)[which][1]).wait_send()
        return carry

    lax.fori_loop(0, HEADS, drain, 0)
    for r in range(1, 2 * WIDE):
        weight(r).wait_send()
        weight_twin(r, c).wait_send()


def local(queries, keys, values, query_tan, key_tan, value_tan, out_weight, gate, gate_tan):
    fixed = (queries, keys, values, query_tan, key_tan, value_tan, out_weight.reshape(HEADS, DH, -1))
    fixed = [pltpu.with_memory_space_constraint(array, pltpu.HBM) for array in fixed]
    rows = queries.shape[0]
    width = gate.shape[0]
    dma = pltpu.SemaphoreType.DMA
    hbm = pl.BlockSpec(memory_space=pltpu.HBM)
    vmem = pl.BlockSpec(memory_space=pltpu.VMEM)
    projected = pl.pallas_call(
        functools.partial(kernel, rows, width),
        out_shape=jax.ShapeDtypeStruct((2 * rows, width), F32),
        in_specs=[hbm] * 7,
        out_specs=vmem,
        scratch_shapes=[
            pltpu.VMEM((HEADS, 2, rows, 2 * DH), BF16),
            pltpu.VMEM((RING, HEADS, 2, 2, rows, 2 * DH), BF16),
            pltpu.VMEM((HEADS, 2 * WIDE, DH, width), BF16),
            pltpu.VMEM((HEADS, 2, rows, 2 * WIDE * DH), BF16),
            pltpu.VMEM((2 * rows, DH), F32),
            pltpu.VMEM((2 * rows, DH), F32),
            pltpu.VMEM((2 * rows, DH), F32),
            pltpu.VMEM((2, 2 * rows, DH), F32),
            pltpu.VMEM((2, rows, DH), F32),
            pltpu.VMEM((rows, DH), F32),
            pltpu.VMEM((rows, DH), F32),
            pltpu.VMEM((HEADS, 2, rows, DH), BF16),
            pltpu.VMEM((HEADS, 2, rows, DH), BF16),
            pltpu.VMEM((HEADS, 8, 256), F32),
            pltpu.VMEM((HEADS, 8, 256), F32),
            dma((6 * HEADS + 1,)),
            dma((2,)),
            dma((2, HEADS, 7)),
            dma((2, HEADS, 7)),
            dma((2, HEADS, 7)),
            dma((2, HEADS, 7)),
            dma((2, HEADS)),
            dma((2 * WIDE,)),
            dma((2 * WIDE,)),
            dma((2 * WIDE,)),
            dma((2 * WIDE,)),
            dma((2, HEADS, 2)),
            dma((HEADS, 2 * WIDE)),
            dma((HEADS, 2 * WIDE)),
        ],
        compiler_params=pltpu.CompilerParams(
            collective_id=0, has_side_effects=True, vmem_limit_bytes=40 << 20
        ),
    )(*fixed)
    plain, tan = projected[:rows], projected[rows:]
    update = (gate[None, :] * plain).astype(BF16)
    update_tan = (gate_tan[None, :] * plain + gate[None, :] * tan).astype(BF16)
    return update, update_tan


def solution(mesh):
    token = P("ctx", "head")
    in_specs = (token,) * 6 + (P("head", None), P("head"), P("head"))
    return jax.shard_map(
        local, mesh=mesh, in_specs=in_specs, out_specs=(token, token), check_vma=False
    )
```

```python
import functools
import math

import jax
import jax.numpy as jnp
from jax import lax
from jax.experimental import pallas as pl
from jax.experimental.pallas import tpu as pltpu
from jax.sharding import PartitionSpec as P

DH = 128
HEADS = 3
RING = 8
WIDE = 4
FACTOR = 1.0 / math.sqrt(DH)
BASE2 = FACTOR * math.log2(math.e)
MESH = pl.DeviceIdType.MESH
F32 = jnp.float32
BF16 = jnp.bfloat16
NT = (((1,), (1,)), ((), ()))
NN = (((1,), (0,)), ((), ()))
SEND, TAKE = 0, 1
JOIN, PASS = 2, 3
PLAN = (
    ((SEND, 0, 1, 0), (SEND, 0, 1, 1), (SEND, 1, 1, 0), (TAKE, 0, 1, 0), (SEND, 0, 2, 0), (TAKE, 0, 1, 1), (SEND, 0, 2, 1), (SEND, 1, 1, 1)),
    ((TAKE, 1, 1, 0),),
    (),
    ((TAKE, 0, 2, 0), (SEND, 0, 3, 0), (SEND, 1, 2, 0), (TAKE, 0, 2, 1), (SEND, 0, 3, 1), (TAKE, 1, 1, 1)),
    (),
    ((TAKE, 0, 3, 0), (SEND, 0, 4, 0), (SEND, 1, 2, 1), (SEND, 2, 1, 0), (TAKE, 1, 2, 0), (SEND, 1, 3, 0), (SEND, 2, 1, 1), (TAKE, 0, 3, 1), (TAKE, 0, 4, 0)),
    (),
    ((TAKE, 1, 2, 1), (SEND, 1, 3, 1)),
    (),
    (),
    ((TAKE, 2, 1, 0), (SEND, 2, 2, 0)),
    (),
    (),
    ((TAKE, 1, 3, 0), (SEND, 1, 4, 0), (JOIN, 0), (TAKE, 2, 1, 1), (SEND, 2, 2, 1), (TAKE, 1, 3, 1), (TAKE, 2, 2, 0), (SEND, 2, 3, 0)),
    (),
    ((TAKE, 1, 4, 0), (TAKE, 2, 2, 1), (SEND, 2, 3, 1)),
    ((PASS, 0),),
    ((TAKE, 2, 3, 0), (SEND, 2, 4, 0)),
    (),
    (),
    (),
    ((TAKE, 2, 3, 1), (JOIN, 1), (TAKE, 2, 4, 0)),
    (),
    (),
)


def kernel(
    rows,
    width,
    queries,
    keys,
    values,
    query_tan,
    key_tan,
    value_tan,
    out_weight,
    acc,
    qq,
    kv,
    wbuf,
    abuf,
    top,
    norm,
    slope,
    total,
    own,
    own_lse,
    own_slope,
    part,
    part_got,
    stat,
    stat_got,
    load_sem,
    q_sem,
    ring_send,
    ring_recv,
    sib_send,
    sib_recv,
    first_sem,
    w_send,
    w_recv,
    w_sib_send,
    w_sib_recv,
    part_sem,
    att_send,
    att_recv,
):
    half = rows // 2
    i = lax.axis_index("ctx")
    g = lax.axis_index("head")
    z, y, c = i // 4, (i // 2) % 2, i % 2
    yh, x = g // WIDE, g % WIDE
    ahead = (((z + 1) % RING) * 4 + y * 2 + c, g)
    behind = (((z + RING - 1) % RING) * 4 + y * 2 + c, g)
    sibling = (z * 4 + y * 2 + 1 - c, g)
    partner = (z * 4 + (1 - y) * 2 + c, g)

    def peer(r):
        return (i, ((yh + r // WIDE) % 2) * WIDE + (x + r % WIDE) % WIDE)

    def back(r):
        return (r // WIDE) * WIDE + (WIDE - r % WIDE) % WIDE

    barrier = pltpu.get_barrier_semaphore()
    others = [ahead, behind, sibling, partner] + [peer(r) for r in range(1, 2 * WIDE)]
    for other in others:
        pl.semaphore_signal(barrier, inc=1, device_id=other, device_id_type=MESH)

    loads = []

    def load(src, dst):
        copy = pltpu.make_async_copy(src, dst, load_sem.at[len(loads)])
        copy.start()
        loads.append(copy)

    def cols(h):
        return pl.ds(h * DH, DH)

    def load_keys(h):
        for pair, low, high in ((0, keys, key_tan), (1, values, value_tan)):
            load(low.at[:, cols(h)], kv.at[0, h, pair, c, :, pl.ds(0, DH)])
            load(high.at[:, cols(h)], kv.at[0, h, pair, c, :, pl.ds(DH, DH)])

    load_keys(0)
    for h in range(HEADS):
        load(query_tan.at[:, cols(h)], qq.at[h, 0, :, pl.ds(0, DH)])
        load(queries.at[:, cols(h)], qq.at[h, 0, :, pl.ds(DH, DH)])
    load_keys(1)
    load_keys(2)
    load(out_weight.at[:, :, pl.ds(pl.multiple_of(g * width, 128), width)], wbuf.at[:, 0])

    pl.semaphore_wait(barrier, len(others))

    def remote(src, dst, send, recv, device):
        return pltpu.make_async_remote_copy(
            src_ref=src,
            dst_ref=dst,
            send_sem=send,
            recv_sem=recv,
            device_id=device,
            device_id_type=MESH,
        )

    def slot_of(d, s):
        return 0 if s == 0 else (7 if s == 4 else 2 * s - 1 + d)

    def piece(d, h, s, part_index):
        return kv.at[slot_of(d, s), h, :, c, pl.ds(part_index * half, half)]

    def ring(d, h, s, p):
        tag = 2 * (s - 1) + (p if s < 4 else 0)
        return remote(
            piece(d, h, s - 1, p),
            piece(d, h, s, p),
            ring_send.at[d, h, tag],
            ring_recv.at[d, h, tag],
            ahead if d == 0 else behind,
        )

    def twin(d, h, s, p):
        tag = 2 * (s - 1) + (p if s < 4 else 0)
        ref = piece(d, h, s, p)
        return remote(ref, ref, sib_send.at[d, h, tag], sib_recv.at[d, h, tag], sibling)

    def twin_got(d, h, s, p):
        tag = 2 * (s - 1) + (p if s < 4 else 0)
        ref = kv.at[slot_of(d, s), h, :, 1 - c, pl.ds(p * half, half)]
        return remote(ref, ref, sib_send.at[d, h, tag], sib_recv.at[d, h, tag], sibling)

    def first(h, core):
        ref = kv.at[0, h, :, core]
        return remote(ref, ref, first_sem.at[0, h], first_sem.at[1, h], sibling)

    def query_copy():
        return remote(qq.at[:, 0], qq.at[:, 1], q_sem.at[0], q_sem.at[1], partner)

    share = DH // 2

    def weight(r):
        column = peer(r)[1] * width
        return remote(
            out_weight.at[:, pl.ds(c * share, share), pl.ds(pl.multiple_of(column, 128), width)],
            wbuf.at[:, back(r), pl.ds(c * share, share)],
            w_send.at[r],
            w_recv.at[back(r)],
            peer(r),
        )

    def weight_got(r):
        ref = wbuf.at[:, r, pl.ds(c * share, share)]
        return remote(ref, ref, w_send.at[r], w_recv.at[r], peer(r))

    def weight_twin(r, core):
        ref = wbuf.at[:, r, pl.ds(core * share, share)]
        return remote(ref, ref, w_sib_send.at[r], w_sib_recv.at[r], sibling)

    def part_copies(h, p):
        return (
            remote(
                part.at[h, :, pl.ds(p * half, half)],
                part_got.at[h, :, pl.ds(p * half, half)],
                part_sem.at[0, h, p, 0],
                part_sem.at[1, h, p, 0],
                partner,
            ),
            remote(
                stat.at[h, p],
                stat_got.at[h, p],
                part_sem.at[0, h, p, 1],
                part_sem.at[1, h, p, 1],
                partner,
            ),
        )

    straight = ((0, 4, 4), (0, 2, 2), (0, 1, 3), (0, 3, 1))
    onward = ((4, 1, 7), (4, 3, 5), (2, 4, 6))

    def attention_copy(h, leg, p):
        source, target, lands = leg
        lines = pl.ds(p * half, half)
        return remote(
            abuf.at[h, :, lines, pl.ds(source * DH, DH)],
            abuf.at[h, :, lines, pl.ds(lands * DH, DH)],
            att_send.at[h, lands, p],
            att_recv.at[h, lands, p],
            peer(target),
        )

    def attention_got(h, r, p):
        ref = abuf.at[h, :, pl.ds(p * half, half), pl.ds(r * DH, DH)]
        return remote(ref, ref, att_send.at[h, r, p], att_recv.at[h, r, p], peer(r))

    def order(d):
        return ((d, d), (d, 1 - d))

    def ring_ops(ops):
        waiting = []
        for what, h, *rest in ops:
            if what in (JOIN, PASS):
                for p in range(2):
                    (combine if what == JOIN else hand_on)(h, p)
                continue
            s, which = rest
            if what == TAKE:
                for copy in waiting:
                    copy.start()
                for d in range(2):
                    ring(d, h, s, order(d)[which][1]).wait_recv()
                waiting = [twin(d, h, s, order(d)[which][1]) for d in range(2)]
            else:
                for d in range(2):
                    ring(d, h, s, order(d)[which][1]).start()
        for copy in waiting:
            copy.start()

    def twins_arrived(h, s):
        for d in range(2):
            for which in range(1 if s == 4 else 2):
                twin_got(d, h, s, order(d)[which][1]).wait_recv()

    def attend(h, slot, low=0, high=2):
        lines = slice(low * rows, high * rows)
        q = qq[h, low:high].reshape((high - low) * rows, 2 * DH)
        k = kv[slot, h, 0].reshape(2 * rows, 2 * DH)
        v = kv[slot, h, 1].reshape(2 * rows, 2 * DH)
        scores = lax.dot_general(q[:, DH:], k[:, :DH], NT, preferred_element_type=F32)
        score_tan = lax.dot_general(q, k, NT, preferred_element_type=F32)
        old = top[lines]
        new = jnp.maximum(old, jnp.max(scores, axis=1, keepdims=True))
        top[lines] = new
        alpha = jnp.exp2((old - new) * BASE2)
        weights, mixed = [], []
        for j in range(2 * rows // DH):
            block = slice(j * DH, (j + 1) * DH)
            exponent = jnp.exp2((scores[:, block] - new) * BASE2)
            weights.append(exponent)
            mixed.append(exponent * score_tan[:, block])
        norm[lines] = alpha * norm[lines] + functools.reduce(jnp.add, weights)
        slope[lines] = alpha * slope[lines] + functools.reduce(jnp.add, mixed)
        weights = jnp.concatenate([w.astype(BF16) for w in weights], axis=1)
        mixed = jnp.concatenate([w.astype(BF16) for w in mixed], axis=1)
        plain = lax.dot_general(weights, v, NN, preferred_element_type=F32)
        cross = lax.dot_general(mixed, v[:, :DH], NN, preferred_element_type=F32)
        total[0, lines] = alpha * total[0, lines] + plain[:, :DH]
        total[1, lines] = alpha * total[1, lines] + (plain[:, DH:] + FACTOR * cross)

    def close(low, high):
        lines = slice(low, high)
        normalizer = jnp.sum(norm[lines], axis=1, keepdims=True)
        inverse = 1.0 / normalizer
        slope_mean = FACTOR * jnp.sum(slope[lines], axis=1, keepdims=True) * inverse
        plain = total[0, lines] * inverse
        tan = total[1, lines] * inverse - plain * slope_mean
        return plain, tan, top[lines] * BASE2 + jnp.log2(normalizer), slope_mean

    def finish_partner(h):
        for p in range(2):
            plain, tan, lse, slope_mean = close(rows + p * half, rows + (p + 1) * half)
            part[h, 0, p * half : (p + 1) * half] = plain.astype(BF16)
            part[h, 1, p * half : (p + 1) * half] = tan.astype(BF16)
            lane = lax.broadcasted_iota(jnp.int32, (half, DH), 1)
            both = jnp.where(lane == 0, lse, slope_mean)
            both = jnp.concatenate([both, jnp.zeros((DH - half, DH), F32)], axis=0)
            stat[h, p] = both.T[:8]
            for copy in part_copies(h, p):
                copy.start()

    def finish_own():
        plain, tan, lse, slope_mean = close(0, rows)
        own[0] = plain
        own[1] = tan
        own_lse[...] = lse
        own_slope[...] = jnp.broadcast_to(slope_mean, (rows, DH))

    def combine(h, p):
        for copy in part_copies(h, p):
            copy.wait_recv()
        lines = slice(p * half, (p + 1) * half)
        both = jnp.concatenate([stat_got[h, p], jnp.zeros((DH - 8, DH), F32)], axis=0).T
        lse1, slope1 = both[:half, 0:1], both[:half, 1:2]
        lse0, slope0 = own_lse[lines], own_slope[lines]
        most = jnp.maximum(lse0, lse1)
        e0, e1 = jnp.exp2(lse0 - most), jnp.exp2(lse1 - most)
        inverse = 1.0 / (e0 + e1)
        w0, w1 = e0 * inverse, e1 * inverse
        a0, a1 = own[0, lines], part_got[h, 0, lines].astype(F32)
        t0, t1 = own[1, lines], part_got[h, 1, lines].astype(F32)
        abuf[h, 0, lines, :DH] = (w0 * a0 + w1 * a1).astype(BF16)
        tan = w0 * t0 + w1 * t1 + (w0 * w1) * (slope0 - slope1) * (a0 - a1)
        abuf[h, 1, lines, :DH] = tan.astype(BF16)
        for leg in straight:
            attention_copy(h, leg, p).start()

    def hand_on(h, p):
        attention_got(h, 4, p).wait_recv()
        for leg in onward[:2]:
            attention_copy(h, leg, p).start()
        attention_got(h, 2, p).wait_recv()
        attention_copy(h, onward[2], p).start()

    def project(h, low, high):
        for r in range(low, high):
            if r not in (0, 2, 4):
                for p in range(2):
                    attention_got(h, r, p).wait_recv()
        left = abuf[h, :, :, low * DH : high * DH].reshape(2 * rows, (high - low) * DH)
        right = wbuf[h, low:high].reshape((high - low) * DH, width)
        product = lax.dot_general(left, right, NN, preferred_element_type=F32)
        acc[...] = product if h == 0 else acc[...] + product

    def drain_ring(h):
        first(h, c).wait_send()
        for s in range(1, 5):
            for d in range(2):
                for which in range(1 if s == 4 else 2):
                    ring(d, h, s, order(d)[which][1]).wait_send()
                    twin(d, h, s, order(d)[which][1]).wait_send()

    def drain_weights():
        for r in range(1, 2 * WIDE):
            weight(r).wait_send()
            weight_twin(r, c).wait_send()

    def drain_gather(h, p):
        for leg in straight + onward:
            attention_copy(h, leg, p).wait_send()

    def drain_part(h, p):
        for copy in part_copies(h, p):
            copy.wait_send()

    for copy in loads[:4]:
        copy.wait()
    ring_ops(PLAN[0][:2])
    first(0, c).start()
    for copy in loads[4:10]:
        copy.wait()
    query_copy().start()
    for copy in loads[10:]:
        copy.wait()
    for h in range(1, HEADS):
        first(h, c).start()
    ring_ops(PLAN[0][2:])
    query_copy().wait_recv()

    def step(h, slot, carry):
        t = h * RING + slot

        @pl.when(slot == 0)
        def _():
            top[...] = jnp.full_like(top, -1e30)
            norm[...] = jnp.zeros_like(norm)
            slope[...] = jnp.zeros_like(slope)
            total[...] = jnp.zeros_like(total)
            first(h, 1 - c).wait_recv()

        for when, ops in enumerate(PLAN):
            if 0 < when < HEADS * RING - 1 and when // RING == h and ops:

                @pl.when(t == when)
                def _():
                    ring_ops(ops)

        for s in range(1, 5):

            @pl.when(slot == 2 * s - 1)
            def _():
                twins_arrived(h, s)

        for r, when in ((6, 0), (5, 1), (7, 2), (4, 3), (2, 4), (1, 5), (3, 6)):

            @pl.when(t == when)
            def _():
                weight(r).start()

        @pl.when(t == 18)
        def _():
            for r in range(1, 2 * WIDE):
                weight_got(r).wait_recv()
                weight_twin(r, c).start()

        attend(h, slot)

        @pl.when(slot == 7)
        def _():
            finish_partner(h)
            finish_own()

        return carry

    last = HEADS * RING - 1
    for h in range(HEADS):
        lax.fori_loop(0, RING if h < HEADS - 1 else RING - 1, functools.partial(step, h), 0)
    ring_ops(PLAN[last])
    twins_arrived(2, 4)
    attend(2, 7, 1, 2)
    finish_partner(2)
    attend(2, 7, 0, 1)
    finish_own()
    for r in range(1, 2 * WIDE):
        weight_twin(r, 1 - c).wait_recv()
    project(0, 0, 2 * WIDE)
    for p in range(2):
        hand_on(1, p)
    query_copy().wait_send()
    for h in range(HEADS):
        drain_ring(h)
    drain_weights()
    for p in range(2):
        combine(2, p)
    project(1, 0, 2 * WIDE)
    for p in range(2):
        for h in range(HEADS):
            drain_part(h, p)
        drain_gather(0, p)
        drain_gather(1, p)
    for p in range(2):
        hand_on(2, p)
    project(2, 0, 5)
    project(2, 5, 2 * WIDE)

    for p in range(2):
        drain_gather(2, p)


def local(queries, keys, values, query_tan, key_tan, value_tan, out_weight, gate, gate_tan):
    fixed = (queries, keys, values, query_tan, key_tan, value_tan, out_weight.reshape(HEADS, DH, -1))
    fixed = [pltpu.with_memory_space_constraint(array, pltpu.HBM) for array in fixed]
    rows = queries.shape[0]
    width = gate.shape[0]
    dma = pltpu.SemaphoreType.DMA
    hbm = pl.BlockSpec(memory_space=pltpu.HBM)
    vmem = pl.BlockSpec(memory_space=pltpu.VMEM)
    projected = pl.pallas_call(
        functools.partial(kernel, rows, width),
        out_shape=jax.ShapeDtypeStruct((2 * rows, width), F32),
        in_specs=[hbm] * 7,
        out_specs=vmem,
        scratch_shapes=[
            pltpu.VMEM((HEADS, 2, rows, 2 * DH), BF16),
            pltpu.VMEM((RING, HEADS, 2, 2, rows, 2 * DH), BF16),
            pltpu.VMEM((HEADS, 2 * WIDE, DH, width), BF16),
            pltpu.VMEM((HEADS, 2, rows, 2 * WIDE * DH), BF16),
            pltpu.VMEM((2 * rows, DH), F32),
            pltpu.VMEM((2 * rows, DH), F32),
            pltpu.VMEM((2 * rows, DH), F32),
            pltpu.VMEM((2, 2 * rows, DH), F32),
            pltpu.VMEM((2, rows, DH), F32),
            pltpu.VMEM((rows, DH), F32),
            pltpu.VMEM((rows, DH), F32),
            pltpu.VMEM((HEADS, 2, rows, DH), BF16),
            pltpu.VMEM((HEADS, 2, rows, DH), BF16),
            pltpu.VMEM((HEADS, 2, 8, DH), F32),
            pltpu.VMEM((HEADS, 2, 8, DH), F32),
            dma((6 * HEADS + 1,)),
            dma((2,)),
            dma((2, HEADS, 7)),
            dma((2, HEADS, 7)),
            dma((2, HEADS, 7)),
            dma((2, HEADS, 7)),
            dma((2, HEADS)),
            dma((2 * WIDE,)),
            dma((2 * WIDE,)),
            dma((2 * WIDE,)),
            dma((2 * WIDE,)),
            dma((2, HEADS, 2, 2)),
            dma((HEADS, 2 * WIDE, 2)),
            dma((HEADS, 2 * WIDE, 2)),
        ],
        compiler_params=pltpu.CompilerParams(
            collective_id=0, has_side_effects=True, vmem_limit_bytes=40 << 20
        ),
    )(*fixed)
    plain, tan = projected[:rows], projected[rows:]
    update = (gate[None, :] * plain).astype(BF16)
    update_tan = (gate_tan[None, :] * plain + gate[None, :] * tan).astype(BF16)
    return update, update_tan


def solution(mesh):
    token = P("ctx", "head")
    in_specs = (token,) * 6 + (P("head", None), P("head"), P("head"))
    return jax.shard_map(
        local, mesh=mesh, in_specs=in_specs, out_specs=(token, token), check_vma=False
    )
```

```python
import functools
import math

import jax
import jax.numpy as jnp
from jax import lax
from jax.experimental import pallas as pl
from jax.experimental.pallas import tpu as pltpu
from jax.sharding import PartitionSpec as P

DH = 128
HEADS = 3
RING = 8
WIDE = 4
FACTOR = 1.0 / math.sqrt(DH)
BASE2 = FACTOR * math.log2(math.e)
MESH = pl.DeviceIdType.MESH
F32 = jnp.float32
BF16 = jnp.bfloat16
NT = (((1,), (1,)), ((), ()))
NN = (((1,), (0,)), ((), ()))
SEND, TAKE = 0, 1
JOIN, PASS = 2, 3
PLAN = (
    ((SEND, 0, 1, 0), (SEND, 1, 1, 0), (SEND, 0, 1, 1), (TAKE, 0, 1, 0), (SEND, 0, 2, 0), (SEND, 1, 1, 1), (TAKE, 1, 1, 0)),
    ((TAKE, 0, 1, 1), (SEND, 0, 2, 1), (TAKE, 0, 2, 0), (SEND, 0, 3, 0), (SEND, 2, 1, 0)),
    (),
    ((TAKE, 1, 1, 1), (TAKE, 0, 2, 1), (SEND, 0, 3, 1), (TAKE, 0, 3, 0), (SEND, 0, 4, 0), (SEND, 1, 2, 0), (SEND, 1, 2, 1), (SEND, 2, 1, 1)),
    (),
    ((TAKE, 2, 1, 0), (TAKE, 0, 3, 1), (TAKE, 0, 4, 0)),
    (),
    ((TAKE, 1, 2, 0), (SEND, 1, 3, 0)),
    (),
    (),
    ((TAKE, 1, 2, 1), (SEND, 1, 3, 1), (SEND, 2, 2, 0)),
    ((TAKE, 2, 1, 1),),
    (),
    ((JOIN, 0), (TAKE, 1, 3, 0), (SEND, 1, 4, 0), (SEND, 2, 2, 1), (TAKE, 1, 3, 1), (TAKE, 2, 2, 0), (SEND, 2, 3, 0)),
    (),
    ((TAKE, 1, 4, 0), (TAKE, 2, 2, 1), (SEND, 2, 3, 1)),
    ((PASS, 0),),
    ((TAKE, 2, 3, 0), (SEND, 2, 4, 0)),
    (),
    (),
    (),
    ((TAKE, 2, 3, 1), (JOIN, 1), (TAKE, 2, 4, 0)),
    (),
    (),
)


def kernel(
    rows,
    width,
    queries,
    keys,
    values,
    query_tan,
    key_tan,
    value_tan,
    out_weight,
    acc,
    qq,
    kv,
    wbuf,
    abuf,
    top,
    norm,
    slope,
    total,
    own,
    own_lse,
    own_slope,
    part,
    part_got,
    stat,
    stat_got,
    load_sem,
    q_sem,
    ring_send,
    ring_recv,
    sib_send,
    sib_recv,
    first_sem,
    w_send,
    w_recv,
    w_sib_send,
    w_sib_recv,
    part_sem,
    att_send,
    att_recv,
):
    half = rows // 2
    i = lax.axis_index("ctx")
    g = lax.axis_index("head")
    z, y, c = i // 4, (i // 2) % 2, i % 2
    yh, x = g // WIDE, g % WIDE
    ahead = (((z + 1) % RING) * 4 + y * 2 + c, g)
    behind = (((z + RING - 1) % RING) * 4 + y * 2 + c, g)
    sibling = (z * 4 + y * 2 + 1 - c, g)
    partner = (z * 4 + (1 - y) * 2 + c, g)

    def peer(r):
        return (i, ((yh + r // WIDE) % 2) * WIDE + (x + r % WIDE) % WIDE)

    def back(r):
        return (r // WIDE) * WIDE + (WIDE - r % WIDE) % WIDE

    barrier = pltpu.get_barrier_semaphore()
    others = [ahead, behind, sibling, partner] + [peer(r) for r in range(1, 2 * WIDE)]
    for other in others:
        pl.semaphore_signal(barrier, inc=1, device_id=other, device_id_type=MESH)

    loads = []

    def load(src, dst):
        copy = pltpu.make_async_copy(src, dst, load_sem.at[len(loads)])
        copy.start()
        loads.append(copy)

    def cols(h):
        return pl.ds(h * DH, DH)

    def load_keys(h):
        for pair, low, high in ((0, keys, key_tan), (1, values, value_tan)):
            load(low.at[:, cols(h)], kv.at[0, h, pair, c, :, pl.ds(0, DH)])
            load(high.at[:, cols(h)], kv.at[0, h, pair, c, :, pl.ds(DH, DH)])

    load_keys(0)
    for h in range(HEADS):
        load(query_tan.at[:, cols(h)], qq.at[h, 0, :, pl.ds(0, DH)])
        load(queries.at[:, cols(h)], qq.at[h, 0, :, pl.ds(DH, DH)])
    load_keys(1)
    load_keys(2)
    load(out_weight.at[:, :, pl.ds(pl.multiple_of(g * width, 128), width)], wbuf.at[:, 0])

    pl.semaphore_wait(barrier, len(others))

    def remote(src, dst, send, recv, device):
        return pltpu.make_async_remote_copy(
            src_ref=src,
            dst_ref=dst,
            send_sem=send,
            recv_sem=recv,
            device_id=device,
            device_id_type=MESH,
        )

    def slot_of(d, s):
        return 0 if s == 0 else (7 if s == 4 else 2 * s - 1 + d)

    def piece(d, h, s, part_index):
        return kv.at[slot_of(d, s), h, :, c, pl.ds(part_index * half, half)]

    def ring(d, h, s, p):
        tag = 2 * (s - 1) + (p if s < 4 else 0)
        return remote(
            piece(d, h, s - 1, p),
            piece(d, h, s, p),
            ring_send.at[d, h, tag],
            ring_recv.at[d, h, tag],
            ahead if d == 0 else behind,
        )

    def twin(d, h, s, p):
        tag = 2 * (s - 1) + (p if s < 4 else 0)
        ref = piece(d, h, s, p)
        return remote(ref, ref, sib_send.at[d, h, tag], sib_recv.at[d, h, tag], sibling)

    def twin_got(d, h, s, p):
        tag = 2 * (s - 1) + (p if s < 4 else 0)
        ref = kv.at[slot_of(d, s), h, :, 1 - c, pl.ds(p * half, half)]
        return remote(ref, ref, sib_send.at[d, h, tag], sib_recv.at[d, h, tag], sibling)

    def first(h, core):
        ref = kv.at[0, h, :, core]
        return remote(ref, ref, first_sem.at[0, h], first_sem.at[1, h], sibling)

    def query_copy():
        return remote(qq.at[:, 0], qq.at[:, 1], q_sem.at[0], q_sem.at[1], partner)

    share = DH // 2

    def weight(r):
        column = peer(r)[1] * width
        return remote(
            out_weight.at[:, pl.ds(c * share, share), pl.ds(pl.multiple_of(column, 128), width)],
            wbuf.at[:, back(r), pl.ds(c * share, share)],
            w_send.at[r],
            w_recv.at[back(r)],
            peer(r),
        )

    def weight_got(r):
        ref = wbuf.at[:, r, pl.ds(c * share, share)]
        return remote(ref, ref, w_send.at[r], w_recv.at[r], peer(r))

    def weight_twin(r, core):
        ref = wbuf.at[:, r, pl.ds(core * share, share)]
        return remote(ref, ref, w_sib_send.at[r], w_sib_recv.at[r], sibling)

    def part_copies(h, p):
        return (
            remote(
                part.at[h, :, pl.ds(p * half, half)],
                part_got.at[h, :, pl.ds(p * half, half)],
                part_sem.at[0, h, p, 0],
                part_sem.at[1, h, p, 0],
                partner,
            ),
            remote(
                stat.at[h, p],
                stat_got.at[h, p],
                part_sem.at[0, h, p, 1],
                part_sem.at[1, h, p, 1],
                partner,
            ),
        )

    straight = ((0, 4, 4), (0, 2, 2), (0, 1, 3), (0, 3, 1))
    onward = ((4, 1, 7), (4, 3, 5), (2, 4, 6))

    def attention_copy(h, leg, p):
        source, target, lands = leg
        lines = pl.ds(p * half, half)
        return remote(
            abuf.at[h, :, lines, pl.ds(source * DH, DH)],
            abuf.at[h, :, lines, pl.ds(lands * DH, DH)],
            att_send.at[h, lands, p],
            att_recv.at[h, lands, p],
            peer(target),
        )

    def attention_got(h, r, p):
        ref = abuf.at[h, :, pl.ds(p * half, half), pl.ds(r * DH, DH)]
        return remote(ref, ref, att_send.at[h, r, p], att_recv.at[h, r, p], peer(r))

    def order(d):
        return ((d, d), (d, 1 - d))

    def ring_ops(ops):
        waiting = []
        for what, h, *rest in ops:
            if what in (JOIN, PASS):
                for p in range(2):
                    (combine if what == JOIN else hand_on)(h, p)
                continue
            s, which = rest
            if what == TAKE:
                for copy in waiting:
                    copy.start()
                for d in range(2):
                    ring(d, h, s, order(d)[which][1]).wait_recv()
                waiting = [twin(d, h, s, order(d)[which][1]) for d in range(2)]
            else:
                for d in range(2):
                    ring(d, h, s, order(d)[which][1]).start()
        for copy in waiting:
            copy.start()

    def twins_arrived(h, s):
        for d in range(2):
            for which in range(1 if s == 4 else 2):
                twin_got(d, h, s, order(d)[which][1]).wait_recv()

    def attend(h, slot, low=0, high=2):
        lines = slice(low * rows, high * rows)
        q = qq[h, low:high].reshape((high - low) * rows, 2 * DH)
        k = kv[slot, h, 0].reshape(2 * rows, 2 * DH)
        v = kv[slot, h, 1].reshape(2 * rows, 2 * DH)
        scores = lax.dot_general(q[:, DH:], k[:, :DH], NT, preferred_element_type=F32)
        score_tan = lax.dot_general(q, k, NT, preferred_element_type=F32)
        old = top[lines]
        new = jnp.maximum(old, jnp.max(scores, axis=1, keepdims=True))
        top[lines] = new
        alpha = jnp.exp2((old - new) * BASE2)
        weights, mixed = [], []
        for j in range(2 * rows // DH):
            block = slice(j * DH, (j + 1) * DH)
            exponent = jnp.exp2((scores[:, block] - new) * BASE2)
            weights.append(exponent)
            mixed.append(exponent * score_tan[:, block])
        norm[lines] = alpha * norm[lines] + functools.reduce(jnp.add, weights)
        slope[lines] = alpha * slope[lines] + functools.reduce(jnp.add, mixed)
        weights = jnp.concatenate([w.astype(BF16) for w in weights], axis=1)
        mixed = jnp.concatenate([w.astype(BF16) for w in mixed], axis=1)
        plain = lax.dot_general(weights, v, NN, preferred_element_type=F32)
        cross = lax.dot_general(mixed, v[:, :DH], NN, preferred_element_type=F32)
        total[0, lines] = alpha * total[0, lines] + plain[:, :DH]
        total[1, lines] = alpha * total[1, lines] + (plain[:, DH:] + FACTOR * cross)

    def close(low, high):
        lines = slice(low, high)
        normalizer = jnp.sum(norm[lines], axis=1, keepdims=True)
        inverse = 1.0 / normalizer
        slope_mean = FACTOR * jnp.sum(slope[lines], axis=1, keepdims=True) * inverse
        plain = total[0, lines] * inverse
        tan = total[1, lines] * inverse - plain * slope_mean
        return plain, tan, top[lines] * BASE2 + jnp.log2(normalizer), slope_mean

    def finish_partner(h):
        for p in range(2):
            plain, tan, lse, slope_mean = close(rows + p * half, rows + (p + 1) * half)
            part[h, 0, p * half : (p + 1) * half] = plain.astype(BF16)
            part[h, 1, p * half : (p + 1) * half] = tan.astype(BF16)
            lane = lax.broadcasted_iota(jnp.int32, (half, DH), 1)
            both = jnp.where(lane == 0, lse, slope_mean)
            both = jnp.concatenate([both, jnp.zeros((DH - half, DH), F32)], axis=0)
            stat[h, p] = both.T[:8]
            for copy in part_copies(h, p):
                copy.start()

    def finish_own():
        plain, tan, lse, slope_mean = close(0, rows)
        own[0] = plain
        own[1] = tan
        own_lse[...] = lse
        own_slope[...] = jnp.broadcast_to(slope_mean, (rows, DH))

    def combine(h, p):
        for copy in part_copies(h, p):
            copy.wait_recv()
        lines = slice(p * half, (p + 1) * half)
        both = jnp.concatenate([stat_got[h, p], jnp.zeros((DH - 8, DH), F32)], axis=0).T
        lse1, slope1 = both[:half, 0:1], both[:half, 1:2]
        lse0, slope0 = own_lse[lines], own_slope[lines]
        most = jnp.maximum(lse0, lse1)
        e0, e1 = jnp.exp2(lse0 - most), jnp.exp2(lse1 - most)
        inverse = 1.0 / (e0 + e1)
        w0, w1 = e0 * inverse, e1 * inverse
        a0, a1 = own[0, lines], part_got[h, 0, lines].astype(F32)
        t0, t1 = own[1, lines], part_got[h, 1, lines].astype(F32)
        abuf[h, 0, lines, :DH] = (w0 * a0 + w1 * a1).astype(BF16)
        tan = w0 * t0 + w1 * t1 + (w0 * w1) * (slope0 - slope1) * (a0 - a1)
        abuf[h, 1, lines, :DH] = tan.astype(BF16)
        for leg in straight:
            attention_copy(h, leg, p).start()

    def hand_on(h, p):
        attention_got(h, 4, p).wait_recv()
        for leg in onward[:2]:
            attention_copy(h, leg, p).start()
        attention_got(h, 2, p).wait_recv()
        attention_copy(h, onward[2], p).start()

    def project(h, low, high):
        for r in range(low, high):
            if r not in (0, 2, 4):
                for p in range(2):
                    attention_got(h, r, p).wait_recv()
        left = abuf[h, :, :, low * DH : high * DH].reshape(2 * rows, (high - low) * DH)
        right = wbuf[h, low:high].reshape((high - low) * DH, width)
        product = lax.dot_general(left, right, NN, preferred_element_type=F32)
        acc[...] = product if h == 0 else acc[...] + product

    def drain_ring(h):
        first(h, c).wait_send()
        for s in range(1, 5):
            for d in range(2):
                for which in range(1 if s == 4 else 2):
                    ring(d, h, s, order(d)[which][1]).wait_send()
                    twin(d, h, s, order(d)[which][1]).wait_send()

    def drain_weights():
        for r in range(1, 2 * WIDE):
            weight(r).wait_send()
            weight_twin(r, c).wait_send()

    def drain_gather(h, p):
        for leg in straight + onward:
            attention_copy(h, leg, p).wait_send()

    def drain_part(h, p):
        for copy in part_copies(h, p):
            copy.wait_send()

    for copy in loads[:4]:
        copy.wait()
    ring_ops(PLAN[0][:1])
    first(0, c).start()
    for copy in loads[4:10]:
        copy.wait()
    query_copy().start()
    for copy in loads[10:]:
        copy.wait()
    for h in range(1, HEADS):
        first(h, c).start()
    ring_ops(PLAN[0][1:])
    query_copy().wait_recv()

    def step(h, slot, carry):
        t = h * RING + slot

        @pl.when(slot == 0)
        def _():
            top[...] = jnp.full_like(top, -1e30)
            norm[...] = jnp.zeros_like(norm)
            slope[...] = jnp.zeros_like(slope)
            total[...] = jnp.zeros_like(total)
            first(h, 1 - c).wait_recv()

        for when, ops in enumerate(PLAN):
            if 0 < when < HEADS * RING - 1 and when // RING == h and ops:

                @pl.when(t == when)
                def _():
                    ring_ops(ops)

        for s in range(1, 5):

            @pl.when(slot == 2 * s - 1)
            def _():
                twins_arrived(h, s)

        for r, when in ((6, 0), (5, 1), (7, 2), (4, 3), (2, 4), (1, 5), (3, 6)):

            @pl.when(t == when)
            def _():
                weight(r).start()

        @pl.when(t == 18)
        def _():
            for r in range(1, 2 * WIDE):
                weight_got(r).wait_recv()
                weight_twin(r, c).start()

        attend(h, slot)

        @pl.when(slot == 7)
        def _():
            finish_partner(h)
            finish_own()

        return carry

    last = HEADS * RING - 1
    for h in range(HEADS):
        for slot in range(RING if h < HEADS - 1 else RING - 1):
            step(h, slot, 0)
    ring_ops(PLAN[last])
    twins_arrived(2, 4)
    attend(2, 7, 1, 2)
    finish_partner(2)
    attend(2, 7, 0, 1)
    finish_own()
    for r in range(1, 2 * WIDE):
        weight_twin(r, 1 - c).wait_recv()
    project(0, 0, 2 * WIDE)
    for p in range(2):
        hand_on(1, p)
    query_copy().wait_send()
    for h in range(HEADS):
        drain_ring(h)
    drain_weights()
    for p in range(2):
        combine(2, p)
    project(1, 0, 2 * WIDE)
    for p in range(2):
        for h in range(HEADS):
            drain_part(h, p)
        drain_gather(0, p)
        drain_gather(1, p)
    for p in range(2):
        hand_on(2, p)
    project(2, 0, 5)
    project(2, 5, 2 * WIDE)

    for p in range(2):
        drain_gather(2, p)


def local(queries, keys, values, query_tan, key_tan, value_tan, out_weight, gate, gate_tan):
    fixed = (queries, keys, values, query_tan, key_tan, value_tan, out_weight.reshape(HEADS, DH, -1))
    fixed = [pltpu.with_memory_space_constraint(array, pltpu.HBM) for array in fixed]
    rows = queries.shape[0]
    width = gate.shape[0]
    dma = pltpu.SemaphoreType.DMA
    hbm = pl.BlockSpec(memory_space=pltpu.HBM)
    vmem = pl.BlockSpec(memory_space=pltpu.VMEM)
    projected = pl.pallas_call(
        functools.partial(kernel, rows, width),
        out_shape=jax.ShapeDtypeStruct((2 * rows, width), F32),
        in_specs=[hbm] * 7,
        out_specs=vmem,
        scratch_shapes=[
            pltpu.VMEM((HEADS, 2, rows, 2 * DH), BF16),
            pltpu.VMEM((RING, HEADS, 2, 2, rows, 2 * DH), BF16),
            pltpu.VMEM((HEADS, 2 * WIDE, DH, width), BF16),
            pltpu.VMEM((HEADS, 2, rows, 2 * WIDE * DH), BF16),
            pltpu.VMEM((2 * rows, DH), F32),
            pltpu.VMEM((2 * rows, DH), F32),
            pltpu.VMEM((2 * rows, DH), F32),
            pltpu.VMEM((2, 2 * rows, DH), F32),
            pltpu.VMEM((2, rows, DH), F32),
            pltpu.VMEM((rows, DH), F32),
            pltpu.VMEM((rows, DH), F32),
            pltpu.VMEM((HEADS, 2, rows, DH), BF16),
            pltpu.VMEM((HEADS, 2, rows, DH), BF16),
            pltpu.VMEM((HEADS, 2, 8, DH), F32),
            pltpu.VMEM((HEADS, 2, 8, DH), F32),
            dma((6 * HEADS + 1,)),
            dma((2,)),
            dma((2, HEADS, 7)),
            dma((2, HEADS, 7)),
            dma((2, HEADS, 7)),
            dma((2, HEADS, 7)),
            dma((2, HEADS)),
            dma((2 * WIDE,)),
            dma((2 * WIDE,)),
            dma((2 * WIDE,)),
            dma((2 * WIDE,)),
            dma((2, HEADS, 2, 2)),
            dma((HEADS, 2 * WIDE, 2)),
            dma((HEADS, 2 * WIDE, 2)),
        ],
        compiler_params=pltpu.CompilerParams(
            collective_id=0, has_side_effects=True, vmem_limit_bytes=40 << 20
        ),
    )(*fixed)
    plain, tan = projected[:rows], projected[rows:]
    update = (gate[None, :] * plain).astype(BF16)
    update_tan = (gate_tan[None, :] * plain + gate[None, :] * tan).astype(BF16)
    return update, update_tan


def solution(mesh):
    token = P("ctx", "head")
    in_specs = (token,) * 6 + (P("head", None), P("head"), P("head"))
    return jax.shard_map(
        local, mesh=mesh, in_specs=in_specs, out_specs=(token, token), check_vma=False
    )
```

```python
import functools
import math

import jax
import jax.numpy as jnp
from jax import lax
from jax.experimental import pallas as pl
from jax.experimental.pallas import tpu as pltpu
from jax.sharding import PartitionSpec as P

DH = 128
HEADS = 3
RING = 8
WIDE = 4
FACTOR = 1.0 / math.sqrt(DH)
BASE2 = FACTOR * math.log2(math.e)
MESH = pl.DeviceIdType.MESH
F32 = jnp.float32
BF16 = jnp.bfloat16
NT = (((1,), (1,)), ((), ()))
NN = (((1,), (0,)), ((), ()))
SEND, TAKE = 0, 1
JOIN, PASS = 2, 3
PLAN = (
    ((SEND, 0, 1, 0), (SEND, 1, 1, 0), (SEND, 0, 1, 1), (TAKE, 0, 1, 0), (SEND, 0, 2, 0), (SEND, 1, 1, 1), (TAKE, 1, 1, 0)),
    ((TAKE, 0, 1, 1), (SEND, 0, 2, 1), (TAKE, 0, 2, 0), (SEND, 0, 3, 0), (SEND, 2, 1, 0)),
    (),
    ((TAKE, 1, 1, 1), (TAKE, 0, 2, 1), (SEND, 0, 3, 1), (TAKE, 0, 3, 0), (SEND, 0, 4, 0), (SEND, 1, 2, 0), (SEND, 1, 2, 1), (SEND, 2, 1, 1)),
    (),
    ((TAKE, 2, 1, 0), (TAKE, 0, 3, 1), (TAKE, 0, 4, 0)),
    (),
    ((TAKE, 1, 2, 0), (SEND, 1, 3, 0)),
    (),
    (),
    ((TAKE, 1, 2, 1), (SEND, 1, 3, 1), (SEND, 2, 2, 0)),
    ((TAKE, 2, 1, 1),),
    (),
    ((JOIN, 0), (TAKE, 1, 3, 0), (SEND, 1, 4, 0), (SEND, 2, 2, 1), (TAKE, 1, 3, 1), (TAKE, 2, 2, 0), (SEND, 2, 3, 0)),
    (),
    ((TAKE, 1, 4, 0), (TAKE, 2, 2, 1), (SEND, 2, 3, 1)),
    ((PASS, 0),),
    ((TAKE, 2, 3, 0), (SEND, 2, 4, 0)),
    (),
    (),
    (),
    ((TAKE, 2, 3, 1), (JOIN, 1), (TAKE, 2, 4, 0)),
    (),
    (),
)


def kernel(
    rows,
    width,
    queries,
    keys,
    values,
    query_tan,
    key_tan,
    value_tan,
    out_weight,
    acc,
    qq,
    kv,
    wbuf,
    abuf,
    top,
    norm,
    slope,
    total,
    own,
    own_lse,
    own_slope,
    part,
    part_got,
    stat,
    stat_got,
    load_sem,
    q_sem,
    ring_send,
    ring_recv,
    sib_send,
    sib_recv,
    first_sem,
    w_send,
    w_recv,
    w_sib_send,
    w_sib_recv,
    part_sem,
    att_send,
    att_recv,
):
    half = rows // 2
    i = lax.axis_index("ctx")
    g = lax.axis_index("head")
    z, y, c = i // 4, (i // 2) % 2, i % 2
    yh, x = g // WIDE, g % WIDE
    ahead = (((z + 1) % RING) * 4 + y * 2 + c, g)
    behind = (((z + RING - 1) % RING) * 4 + y * 2 + c, g)
    sibling = (z * 4 + y * 2 + 1 - c, g)
    partner = (z * 4 + (1 - y) * 2 + c, g)

    def peer(r):
        return (i, ((yh + r // WIDE) % 2) * WIDE + (x + r % WIDE) % WIDE)

    def back(r):
        return (r // WIDE) * WIDE + (WIDE - r % WIDE) % WIDE

    barrier = pltpu.get_barrier_semaphore()
    others = [ahead, behind, sibling, partner] + [peer(r) for r in range(1, 2 * WIDE)]
    for other in others:
        pl.semaphore_signal(barrier, inc=1, device_id=other, device_id_type=MESH)

    loads = []

    def load(src, dst):
        copy = pltpu.make_async_copy(src, dst, load_sem.at[len(loads)])
        copy.start()
        loads.append(copy)

    def cols(h):
        return pl.ds(h * DH, DH)

    def load_keys(h):
        for pair, low, high in ((0, keys, key_tan), (1, values, value_tan)):
            load(low.at[:, cols(h)], kv.at[0, h, pair, c, :, pl.ds(0, DH)])
            load(high.at[:, cols(h)], kv.at[0, h, pair, c, :, pl.ds(DH, DH)])

    load_keys(0)
    for h in range(HEADS):
        load(query_tan.at[:, cols(h)], qq.at[h, 0, :, pl.ds(0, DH)])
        load(queries.at[:, cols(h)], qq.at[h, 0, :, pl.ds(DH, DH)])
    load_keys(1)
    load_keys(2)
    load(out_weight.at[:, :, pl.ds(pl.multiple_of(g * width, 128), width)], wbuf.at[:, 0])

    pl.semaphore_wait(barrier, len(others))

    def remote(src, dst, send, recv, device):
        return pltpu.make_async_remote_copy(
            src_ref=src,
            dst_ref=dst,
            send_sem=send,
            recv_sem=recv,
            device_id=device,
            device_id_type=MESH,
        )

    def slot_of(d, s):
        return 0 if s == 0 else (7 if s == 4 else 2 * s - 1 + d)

    def piece(d, h, s, part_index):
        return kv.at[slot_of(d, s), h, :, c, pl.ds(part_index * half, half)]

    def ring(d, h, s, p):
        tag = 2 * (s - 1) + (p if s < 4 else 0)
        return remote(
            piece(d, h, s - 1, p),
            piece(d, h, s, p),
            ring_send.at[d, h, tag],
            ring_recv.at[d, h, tag],
            ahead if d == 0 else behind,
        )

    def twin(d, h, s, p):
        tag = 2 * (s - 1) + (p if s < 4 else 0)
        ref = piece(d, h, s, p)
        return remote(ref, ref, sib_send.at[d, h, tag], sib_recv.at[d, h, tag], sibling)

    def twin_got(d, h, s, p):
        tag = 2 * (s - 1) + (p if s < 4 else 0)
        ref = kv.at[slot_of(d, s), h, :, 1 - c, pl.ds(p * half, half)]
        return remote(ref, ref, sib_send.at[d, h, tag], sib_recv.at[d, h, tag], sibling)

    def first(h, core):
        ref = kv.at[0, h, :, core]
        return remote(ref, ref, first_sem.at[0, h], first_sem.at[1, h], sibling)

    def query_copy():
        return remote(qq.at[:, 0], qq.at[:, 1], q_sem.at[0], q_sem.at[1], partner)

    share = DH // 2

    def weight(r):
        column = peer(r)[1] * width
        return remote(
            out_weight.at[:, pl.ds(c * share, share), pl.ds(pl.multiple_of(column, 128), width)],
            wbuf.at[:, back(r), pl.ds(c * share, share)],
            w_send.at[r],
            w_recv.at[back(r)],
            peer(r),
        )

    def weight_got(r):
        ref = wbuf.at[:, r, pl.ds(c * share, share)]
        return remote(ref, ref, w_send.at[r], w_recv.at[r], peer(r))

    def weight_twin(r, core):
        ref = wbuf.at[:, r, pl.ds(core * share, share)]
        return remote(ref, ref, w_sib_send.at[r], w_sib_recv.at[r], sibling)

    def part_copies(h, p):
        return (
            remote(
                part.at[h, :, pl.ds(p * half, half)],
                part_got.at[h, :, pl.ds(p * half, half)],
                part_sem.at[0, h, p, 0],
                part_sem.at[1, h, p, 0],
                partner,
            ),
            remote(
                stat.at[h, p],
                stat_got.at[h, p],
                part_sem.at[0, h, p, 1],
                part_sem.at[1, h, p, 1],
                partner,
            ),
        )

    straight = ((0, 4, 4), (0, 2, 2), (0, 1, 3), (0, 3, 1))
    onward = ((4, 1, 7), (4, 3, 5), (2, 4, 6))

    def attention_copy(h, leg, p):
        source, target, lands = leg
        lines = pl.ds(p * half, half)
        return remote(
            abuf.at[h, :, lines, pl.ds(source * DH, DH)],
            abuf.at[h, :, lines, pl.ds(lands * DH, DH)],
            att_send.at[h, lands, p],
            att_recv.at[h, lands, p],
            peer(target),
        )

    def attention_got(h, r, p):
        ref = abuf.at[h, :, pl.ds(p * half, half), pl.ds(r * DH, DH)]
        return remote(ref, ref, att_send.at[h, r, p], att_recv.at[h, r, p], peer(r))

    def order(d):
        return ((d, d), (d, 1 - d))

    def ring_ops(ops):
        waiting = []
        for what, h, *rest in ops:
            if what in (JOIN, PASS):
                for p in range(2):
                    (combine if what == JOIN else hand_on)(h, p)
                continue
            s, which = rest
            if what == TAKE:
                for copy in waiting:
                    copy.start()
                for d in range(2):
                    ring(d, h, s, order(d)[which][1]).wait_recv()
                waiting = [twin(d, h, s, order(d)[which][1]) for d in range(2)]
            else:
                for d in range(2):
                    ring(d, h, s, order(d)[which][1]).start()
        for copy in waiting:
            copy.start()

    def twins_arrived(h, s):
        for d in range(2):
            for which in range(1 if s == 4 else 2):
                twin_got(d, h, s, order(d)[which][1]).wait_recv()

    def attend(h, slot, low=0, high=2):
        lines = slice(low * rows, high * rows)
        q = qq[h, low:high].reshape((high - low) * rows, 2 * DH)
        k = kv[slot, h, 0].reshape(2 * rows, 2 * DH)
        v = kv[slot, h, 1].reshape(2 * rows, 2 * DH)
        scores = lax.dot_general(q[:, DH:], k[:, :DH], NT, preferred_element_type=F32)
        score_tan = lax.dot_general(q, k, NT, preferred_element_type=F32)
        old = top[lines]
        new = jnp.maximum(old, jnp.max(scores, axis=1, keepdims=True))
        top[lines] = new
        alpha = jnp.exp2((old - new) * BASE2)
        weights, mixed = [], []
        for j in range(2 * rows // DH):
            block = slice(j * DH, (j + 1) * DH)
            exponent = jnp.exp2((scores[:, block] - new) * BASE2)
            weights.append(exponent)
            mixed.append(exponent * score_tan[:, block])
        norm[lines] = alpha * norm[lines] + functools.reduce(jnp.add, weights)
        slope[lines] = alpha * slope[lines] + functools.reduce(jnp.add, mixed)
        weights = jnp.concatenate([w.astype(BF16) for w in weights], axis=1)
        mixed = jnp.concatenate([w.astype(BF16) for w in mixed], axis=1)
        plain = lax.dot_general(weights, v, NN, preferred_element_type=F32)
        cross = lax.dot_general(mixed, v[:, :DH], NN, preferred_element_type=F32)
        total[0, lines] = alpha * total[0, lines] + plain[:, :DH]
        total[1, lines] = alpha * total[1, lines] + (plain[:, DH:] + FACTOR * cross)

    def close(low, high):
        lines = slice(low, high)
        normalizer = jnp.sum(norm[lines], axis=1, keepdims=True)
        inverse = 1.0 / normalizer
        slope_mean = FACTOR * jnp.sum(slope[lines], axis=1, keepdims=True) * inverse
        plain = total[0, lines] * inverse
        tan = total[1, lines] * inverse - plain * slope_mean
        return plain, tan, top[lines] * BASE2 + jnp.log2(normalizer), slope_mean

    def finish_partner(h):
        for p in range(2):
            plain, tan, lse, slope_mean = close(rows + p * half, rows + (p + 1) * half)
            part[h, 0, p * half : (p + 1) * half] = plain.astype(BF16)
            part[h, 1, p * half : (p + 1) * half] = tan.astype(BF16)
            lane = lax.broadcasted_iota(jnp.int32, (half, DH), 1)
            both = jnp.where(lane == 0, lse, slope_mean)
            both = jnp.concatenate([both, jnp.zeros((DH - half, DH), F32)], axis=0)
            stat[h, p] = both.T[:8]
            for copy in part_copies(h, p):
                copy.start()

    def finish_own():
        plain, tan, lse, slope_mean = close(0, rows)
        own[0] = plain
        own[1] = tan
        own_lse[...] = lse
        own_slope[...] = jnp.broadcast_to(slope_mean, (rows, DH))

    def combine(h, p):
        for copy in part_copies(h, p):
            copy.wait_recv()
        lines = slice(p * half, (p + 1) * half)
        both = jnp.concatenate([stat_got[h, p], jnp.zeros((DH - 8, DH), F32)], axis=0).T
        lse1, slope1 = both[:half, 0:1], both[:half, 1:2]
        lse0, slope0 = own_lse[lines], own_slope[lines]
        most = jnp.maximum(lse0, lse1)
        e0, e1 = jnp.exp2(lse0 - most), jnp.exp2(lse1 - most)
        inverse = 1.0 / (e0 + e1)
        w0, w1 = e0 * inverse, e1 * inverse
        a0, a1 = own[0, lines], part_got[h, 0, lines].astype(F32)
        t0, t1 = own[1, lines], part_got[h, 1, lines].astype(F32)
        abuf[h, 0, lines, :DH] = (w0 * a0 + w1 * a1).astype(BF16)
        tan = w0 * t0 + w1 * t1 + (w0 * w1) * (slope0 - slope1) * (a0 - a1)
        abuf[h, 1, lines, :DH] = tan.astype(BF16)
        for leg in straight:
            attention_copy(h, leg, p).start()

    def hand_on_x(h, p):
        attention_got(h, 4, p).wait_recv()
        for leg in onward[:2]:
            attention_copy(h, leg, p).start()

    def hand_on_y(h, p):
        attention_got(h, 2, p).wait_recv()
        attention_copy(h, onward[2], p).start()

    def hand_on(h, p):
        hand_on_x(h, p)
        hand_on_y(h, p)

    def project(h, low, high):
        for r in range(low, high):
            if r not in (0, 2, 4):
                for p in range(2):
                    attention_got(h, r, p).wait_recv()
        left = abuf[h, :, :, low * DH : high * DH].reshape(2 * rows, (high - low) * DH)
        right = wbuf[h, low:high].reshape((high - low) * DH, width)
        product = lax.dot_general(left, right, NN, preferred_element_type=F32)
        acc[...] = product if h == 0 else acc[...] + product

    def drain_ring(h):
        first(h, c).wait_send()
        for s in range(1, 5):
            for d in range(2):
                for which in range(1 if s == 4 else 2):
                    ring(d, h, s, order(d)[which][1]).wait_send()
                    twin(d, h, s, order(d)[which][1]).wait_send()

    def drain_weights():
        for r in range(1, 2 * WIDE):
            weight(r).wait_send()
            weight_twin(r, c).wait_send()

    def drain_gather(h, p):
        for leg in straight + onward:
            attention_copy(h, leg, p).wait_send()

    def drain_part(h, p):
        for copy in part_copies(h, p):
            copy.wait_send()

    for copy in loads[:4]:
        copy.wait()
    ring_ops(PLAN[0][:1])
    first(0, c).start()
    for copy in loads[4:10]:
        copy.wait()
    query_copy().start()
    for copy in loads[10:]:
        copy.wait()
    for h in range(1, HEADS):
        first(h, c).start()
    ring_ops(PLAN[0][1:])
    query_copy().wait_recv()

    def step(h, slot, carry):
        t = h * RING + slot

        @pl.when(slot == 0)
        def _():
            top[...] = jnp.full_like(top, -1e30)
            norm[...] = jnp.zeros_like(norm)
            slope[...] = jnp.zeros_like(slope)
            total[...] = jnp.zeros_like(total)
            first(h, 1 - c).wait_recv()

        for when, ops in enumerate(PLAN):
            if 0 < when < HEADS * RING - 1 and when // RING == h and ops:

                @pl.when(t == when)
                def _():
                    ring_ops(ops)

        for s in range(1, 5):

            @pl.when(slot == 2 * s - 1)
            def _():
                twins_arrived(h, s)

        for r, when in ((6, 0), (5, 1), (7, 2), (4, 3), (2, 4), (1, 5), (3, 6)):

            @pl.when(t == when)
            def _():
                weight(r).start()

        @pl.when(t == 18)
        def _():
            for r in range(1, 2 * WIDE):
                weight_got(r).wait_recv()
                weight_twin(r, c).start()

        attend(h, slot)

        @pl.when(slot == 7)
        def _():
            finish_partner(h)
            finish_own()

        return carry

    last = HEADS * RING - 1
    for h in range(HEADS):
        for slot in range(RING if h < HEADS - 1 else RING - 1):
            step(h, slot, 0)
    ring_ops(PLAN[last])
    twins_arrived(2, 4)
    attend(2, 7, 1, 2)
    finish_partner(2)
    attend(2, 7, 0, 1)
    finish_own()
    for r in range(1, 2 * WIDE):
        weight_twin(r, 1 - c).wait_recv()
    project(0, 0, 2 * WIDE)
    for p in range(2):
        hand_on(1, p)
    query_copy().wait_send()
    for h in range(HEADS):
        drain_ring(h)
    drain_weights()
    for p in range(2):
        combine(2, p)
    project(1, 0, 2 * WIDE)
    for p in range(2):
        for h in range(HEADS):
            drain_part(h, p)
        drain_gather(0, p)
        drain_gather(1, p)
    for p in range(2):
        hand_on_x(2, p)
    for p in range(2):
        hand_on_y(2, p)
    project(2, 0, 5)
    project(2, 5, 2 * WIDE)

    for p in range(2):
        drain_gather(2, p)


def local(queries, keys, values, query_tan, key_tan, value_tan, out_weight, gate, gate_tan):
    fixed = (queries, keys, values, query_tan, key_tan, value_tan, out_weight.reshape(HEADS, DH, -1))
    fixed = [pltpu.with_memory_space_constraint(array, pltpu.HBM) for array in fixed]
    rows = queries.shape[0]
    width = gate.shape[0]
    dma = pltpu.SemaphoreType.DMA
    hbm = pl.BlockSpec(memory_space=pltpu.HBM)
    vmem = pl.BlockSpec(memory_space=pltpu.VMEM)
    projected = pl.pallas_call(
        functools.partial(kernel, rows, width),
        out_shape=jax.ShapeDtypeStruct((2 * rows, width), F32),
        in_specs=[hbm] * 7,
        out_specs=vmem,
        scratch_shapes=[
            pltpu.VMEM((HEADS, 2, rows, 2 * DH), BF16),
            pltpu.VMEM((RING, HEADS, 2, 2, rows, 2 * DH), BF16),
            pltpu.VMEM((HEADS, 2 * WIDE, DH, width), BF16),
            pltpu.VMEM((HEADS, 2, rows, 2 * WIDE * DH), BF16),
            pltpu.VMEM((2 * rows, DH), F32),
            pltpu.VMEM((2 * rows, DH), F32),
            pltpu.VMEM((2 * rows, DH), F32),
            pltpu.VMEM((2, 2 * rows, DH), F32),
            pltpu.VMEM((2, rows, DH), F32),
            pltpu.VMEM((rows, DH), F32),
            pltpu.VMEM((rows, DH), F32),
            pltpu.VMEM((HEADS, 2, rows, DH), BF16),
            pltpu.VMEM((HEADS, 2, rows, DH), BF16),
            pltpu.VMEM((HEADS, 2, 8, DH), F32),
            pltpu.VMEM((HEADS, 2, 8, DH), F32),
            dma((6 * HEADS + 1,)),
            dma((2,)),
            dma((2, HEADS, 7)),
            dma((2, HEADS, 7)),
            dma((2, HEADS, 7)),
            dma((2, HEADS, 7)),
            dma((2, HEADS)),
            dma((2 * WIDE,)),
            dma((2 * WIDE,)),
            dma((2 * WIDE,)),
            dma((2 * WIDE,)),
            dma((2, HEADS, 2, 2)),
            dma((HEADS, 2 * WIDE, 2)),
            dma((HEADS, 2 * WIDE, 2)),
        ],
        compiler_params=pltpu.CompilerParams(
            collective_id=0, has_side_effects=True, vmem_limit_bytes=40 << 20
        ),
    )(*fixed)
    plain, tan = projected[:rows], projected[rows:]
    update = (gate[None, :] * plain).astype(BF16)
    update_tan = (gate_tan[None, :] * plain + gate[None, :] * tan).astype(BF16)
    return update, update_tan


def solution(mesh):
    token = P("ctx", "head")
    in_specs = (token,) * 6 + (P("head", None), P("head"), P("head"))
    return jax.shard_map(
        local, mesh=mesh, in_specs=in_specs, out_specs=(token, token), check_vma=False
    )
```
